256 devices in a mesh: tp: 16 (over x, z_lo, core), grp: 16 (over z_hi, y).
Axes of the slice: x: 4, y: 4, z: 8 (z_hi: 4, z_lo: 2; z = z_hi * 2 + z_lo), core: 2. Of those that a mesh axis runs over, the one named last changes fastest.
Arguments:
- queries: bfloat16 [128, 4, 16384], P('grp', None, 'tp')
- new_keys: bfloat16 [128, 4, 1024], P('grp'), may hold values from -6 to 6
- new_values: bfloat16 [128, 4, 1024], P('grp'), may hold values from -6 to 6
- cache_keys: bfloat16 [128, 8, 4096, 128], P('grp', None, 'tp')
- cache_values: bfloat16 [128, 8, 4096, 128], P('grp', None, 'tp'), may hold values from -6 to 6
- lengths: int32 [128], P('grp'), may hold values from 2 to 4092, as said below
- norm_gain: float32 [16384], P('tp'), may hold values from 0.1 to 1.9
- draft_weight: bfloat16 [16384, 16384], P('tp', 'grp'), may hold values from -0.046875 to 0.046875
- next_hidden: bfloat16 [512, 16384], P('tp', 'grp'), may hold values from -6 to 6
Outputs:
- prediction: bfloat16 [512, 16384], P('tp', 'grp')
- weight_grad: bfloat16 [16384, 16384], P('tp', 'grp')
The draws below stay inside these ranges and needn't reach their ends.
Inputs may be any that keep to these rules, and one draw needn't show every extreme that they name: lengths[r] + 4 <= 4096; some sequence has exactly 4092.
All inputs are finite; a program needn't handle non-finite values.
Results may differ from the reference program's by a relative error of at most 0.024.
Values may be sent and summed in bfloat16 or wider, within the bound.
No kernel may reach another device: no remote copies, remote signals or barrier semaphores. Data moves between devices by JAX's collectives and lax.ppermute only.
A program may use at most 64 MiB of HBM per device.

```python
import math
import jax
import jax.numpy as jnp
from jax import lax

HQ = 128
KVH = 8
HD = 128
STEPS = 4
CACHE = 4096
ROWS = 128
DRAFT_ROWS = 512
N_TP = 16


def anchor_keys(key):
    return jax.random.normal(jax.random.fold_in(key, 500), (ROWS, KVH, HD), jnp.float32)


def draw_cache_keys(key, part):
    anchor = anchor_keys(key)
    key = jax.random.fold_in(key, 1)
    keys = jax.random.normal(key, (ROWS, KVH, CACHE, HD), jnp.float32)
    keys = keys.at[:, :, 0, :].set(anchor)
    return keys.astype(jnp.bfloat16)


def draw_queries(key, part):
    key = jax.random.fold_in(key, 2)
    heads = jax.random.normal(key, (ROWS, STEPS, HQ, HD), jnp.float32)
    return heads.reshape(ROWS, STEPS, HQ * HD).astype(jnp.bfloat16)


def draw_lengths(key, part):
    key = jax.random.fold_in(key, 3)
    drawn = jax.random.randint(key, (ROWS,), 2, CACHE - STEPS + 1, dtype=jnp.int32)
    return drawn.at[0].set(CACHE - STEPS)


def steps_of(stream_key, extent, pieces, low, top_value):
    factor_of = 1.0
    for axis_at, parts in pieces:
        draws = jax.random.uniform(jax.random.fold_in(jax.random.fold_in(stream_key, 6), axis_at), (parts,), jnp.float32, low / len(pieces), top_value / len(pieces))
        factor_of = factor_of * jnp.repeat(jnp.exp(draws), extent[axis_at] // parts).reshape((-1,) + (1,) * (len(extent) - 1 - axis_at))
    return factor_of


def noise(rng, shape, spread, bound, shards=(), held_as=jnp.bfloat16):
    factor_of = steps_of(rng, shape, shards, -0.22, 0.18) if shards else 1.0
    values = jax.random.normal(rng, shape, jnp.float32) * spread * factor_of
    return jnp.minimum(jnp.maximum(values, -bound), bound).astype(held_as)


def setup_inputs(seed: int = 0) -> dict:
    seeds = jax.random.split(jax.random.key(seed), 10)
    return {
        "queries": draw_queries(jax.random.fold_in(seeds[9], 71), 0),
        "new_keys": noise(seeds[1], (ROWS, STEPS, KVH * HD), 1.0, 6.0, ((0, 16),)),
        "new_values": noise(seeds[2], (ROWS, STEPS, KVH * HD), 1.0, 6.0, ((0, 16),)),
        "cache_keys": draw_cache_keys(jax.random.fold_in(seeds[9], 71), 0),
        "cache_values": noise(seeds[4], (ROWS, KVH, CACHE, HD), 1.0, 6.0, ((0, 16), (2, 16))),
        "lengths": draw_lengths(jax.random.fold_in(seeds[9], 71), 0),
        "norm_gain": jnp.clip(1.0 + 0.18 * jax.random.normal(seeds[6], (HQ * HD,), jnp.float32), 0.1, 1.9),
        "draft_weight": noise(seeds[7], (HQ * HD, HQ * HD), (HQ * HD) ** -0.5, 0.046875, ((0, 16), (1, 16))),
        "next_hidden": noise(seeds[8], (DRAFT_ROWS, HQ * HD), 1.0, 6.0, ((0, 16), (1, 16))),
    }


def attend_row(item):
    query, new_key, new_value, cached_keys, cached_values, length = item
    groups = HQ // KVH
    block = CACHE // N_TP
    hi = lax.Precision.HIGHEST
    positions = jnp.arange(CACHE, dtype=jnp.int32)
    slot = positions - length
    onehot = (slot[:, None] == jnp.arange(STEPS, dtype=jnp.int32)[None, :]).astype(jnp.float32)
    written = (slot >= 0) & (slot < STEPS)
    put_keys = jnp.einsum('ps,skd->kpd', onehot, new_key.reshape(STEPS, KVH, HD).astype(jnp.float32), precision=hi)
    put_values = jnp.einsum('ps,skd->kpd', onehot, new_value.reshape(STEPS, KVH, HD).astype(jnp.float32), precision=hi)
    keys = jnp.where(written[None, :, None], put_keys, cached_keys.astype(jnp.float32))
    values = jnp.where(written[None, :, None], put_values, cached_values.astype(jnp.float32))
    heads = query.reshape(STEPS, KVH, groups, HD).astype(jnp.float32)
    scores = jnp.einsum('skgd,kpd->skgp', heads, keys, precision=hi) * (1.0 / math.sqrt(HD))
    valid = positions[None, :] < length + jnp.arange(STEPS, dtype=jnp.int32)[:, None] + 1
    valid = valid[:, None, None, :]
    masked = jnp.where(valid, scores, jnp.float32(-1e+30))
    blocks = masked.reshape(STEPS, KVH, groups, N_TP, block)
    valid_blocks = valid.reshape(STEPS, 1, 1, N_TP, block)
    block_max = lax.optimization_barrier(jnp.max(blocks, axis=-1))
    expo = jnp.where(valid_blocks, jnp.exp(blocks - block_max[..., None]), jnp.float32(0.0))
    block_total = lax.optimization_barrier(jnp.sum(expo, axis=-1))
    probs = expo.astype(jnp.bfloat16).astype(jnp.float32)
    block_acc = jnp.einsum('skgbp,kbpd->skgbd', probs, values.reshape(KVH, N_TP, block, HD), precision=hi)
    top = lax.optimization_barrier(jnp.max(block_max, axis=-1))
    factor = jnp.exp(block_max - top[..., None])
    numer = lax.optimization_barrier(jnp.sum(block_acc * factor[..., None], axis=3))
    denom = lax.optimization_barrier(jnp.sum(block_total * factor, axis=3))
    return (numer / denom[..., None]).reshape(STEPS, HQ * HD)

def reference(queries, new_keys, new_values, cache_keys, cache_values, lengths, norm_gain, draft_weight, next_hidden):
    context = lax.map(attend_row, (queries, new_keys, new_values, cache_keys, cache_values, lengths))
    width = HQ * HD
    flat = context.reshape(ROWS * STEPS, width)
    meansq = lax.optimization_barrier(jnp.sum(flat * flat, axis=1)) / width
    rows = (flat * lax.rsqrt(meansq + 1e-05)[:, None] * norm_gain[None, :]).astype(jnp.bfloat16)
    total = jnp.dot(rows, draft_weight, preferred_element_type=jnp.float32)
    prediction = total.astype(jnp.bfloat16)
    grad_out = ((total - next_hidden.astype(jnp.float32)) / math.sqrt(ROWS * STEPS)).astype(jnp.bfloat16)
    weight_grad = jnp.dot(rows.T, grad_out, preferred_element_type=jnp.float32).astype(jnp.bfloat16)
    return (prediction, weight_grad)
```

```python
import math

import jax
import jax.numpy as jnp
from jax import lax
from jax.sharding import PartitionSpec as P


def split_pieces(x):
    a = x.astype(jnp.bfloat16)
    r = x - a.astype(jnp.float32)
    b = r.astype(jnp.bfloat16)
    c = (r - b.astype(jnp.float32)).astype(jnp.bfloat16)
    return a, b, c


def gather(x, axis):
    n = lax.axis_size(axis)
    return lax.all_to_all(jnp.broadcast_to(x[None], (n,) + x.shape), axis, 0, 0)


def per_device(
    queries,
    new_keys,
    new_values,
    cache_keys,
    cache_values,
    lengths,
    norm_gain,
    draft_weight,
    next_hidden,
):
    tp_count = lax.axis_size("tp")
    tp_place = lax.axis_index("tp")
    seqs, steps, feats = queries.shape
    kv_heads, block, head_size = (cache_keys.shape[1], cache_keys.shape[2], cache_keys.shape[3])
    mine = feats // head_size
    width = feats * tp_count
    q_heads = width // head_size
    groups = q_heads // kv_heads
    share = tp_count // kv_heads
    packed = queries.reshape(seqs, steps, mine, head_size).transpose(0, 2, 1, 3)
    heads = gather(packed, "tp").reshape(kv_heads, share, seqs, mine * steps, head_size)
    positions = tp_place * block + jnp.arange(block, dtype=jnp.int32)
    slot = positions[None, :] - lengths[:, None]
    onehot = (slot[:, :, None] == jnp.arange(steps, dtype=jnp.int32)[None, None, :]).astype(
        jnp.bfloat16
    )
    written = ((slot >= 0) & (slot < steps))[:, None, :, None]
    put_keys = jnp.einsum(
        "rps,rskd->rkpd",
        onehot,
        new_keys.reshape(seqs, steps, kv_heads, head_size),
        preferred_element_type=jnp.float32,
    ).astype(jnp.bfloat16)
    put_values = jnp.einsum(
        "rps,rskd->rkpd",
        onehot,
        new_values.reshape(seqs, steps, kv_heads, head_size),
        preferred_element_type=jnp.float32,
    ).astype(jnp.bfloat16)
    keys = jnp.where(written, put_keys, cache_keys)
    values = jnp.where(written, put_values, cache_values)
    scores = jnp.einsum("karqd,rkpd->rkaqp", heads, keys, preferred_element_type=jnp.float32) * (
        1.0 / math.sqrt(head_size)
    )
    step_of = jnp.arange(mine * steps, dtype=jnp.int32) % steps
    limit = lengths[:, None] + step_of[None, :] + 1
    valid = (positions[None, None, :] < limit[:, :, None])[:, None, None]
    masked = jnp.where(valid, scores, jnp.float32(-1e30))
    top = jnp.max(masked, axis=-1)
    expo = jnp.where(valid, jnp.exp(masked - top[..., None]), jnp.float32(0.0))
    total_e = jnp.sum(expo, axis=-1)
    some = total_e > 0
    acc = jnp.einsum(
        "rkaqp,rkpd->karqd", expo.astype(jnp.bfloat16), values, preferred_element_type=jnp.float32
    )
    safe = jnp.where(some, total_e, 1.0)
    lse = jnp.where(some, top + jnp.log(safe), jnp.float32(-1e30))
    outs = (acc * (1.0 / safe).transpose(1, 2, 0, 3)[..., None]).astype(jnp.bfloat16)
    outs = outs.reshape(tp_count, seqs * mine * steps, head_size)
    lse = lse.transpose(1, 2, 0, 3).reshape(tp_count, seqs * mine * steps)
    pieces = jnp.stack(split_pieces(lse), axis=1).reshape(tp_count, -1, head_size)
    extra = -pieces.shape[1] % 16
    pieces = jnp.pad(pieces, ((0, 0), (0, extra), (0, 0)))
    got = lax.all_to_all(jnp.concatenate([outs, pieces], axis=1), "tp", 0, 0)
    n_rows = seqs * mine * steps
    got_out = got[:, :n_rows].astype(jnp.float32)
    n_piece = 3 * n_rows // head_size
    got_lse = (
        got[:, n_rows : n_rows + n_piece].astype(jnp.float32).reshape(tp_count, 3, n_rows)
    )
    got_lse = got_lse[:, 0] + got_lse[:, 1] + got_lse[:, 2]
    factor = jnp.exp(got_lse - jnp.max(got_lse, axis=0, keepdims=True))
    context = jnp.sum(got_out * factor[..., None], axis=0) / jnp.sum(factor, axis=0)[:, None]
    flat = (
        context.reshape(seqs, mine, steps, head_size)
        .transpose(0, 2, 1, 3)
        .reshape(seqs * steps, feats)
    )
    raw = (flat * norm_gain[None, :]).astype(jnp.bfloat16)
    all_raw = gather(raw, "grp").reshape(-1, feats)
    row_count = all_raw.shape[0]
    own = row_count // tp_count
    plain = all_raw.astype(jnp.float32) * (1.0 / norm_gain)[None, :]
    squares = jnp.sum(plain * plain, axis=1).reshape(tp_count, own)
    sq = jnp.stack(split_pieces(squares), axis=-1)
    sq = jnp.pad(sq, ((0, 0), (0, 0), (0, 128 - 3)))
    partial = jnp.dot(all_raw, draft_weight, preferred_element_type=jnp.float32).astype(
        jnp.bfloat16
    )
    cols = partial.shape[1]
    payload = jnp.concatenate([partial.reshape(tp_count, own, cols), sq], axis=2)
    parts = lax.all_to_all(payload, "tp", 0, 0).astype(jnp.float32)
    summed = jnp.sum(parts, axis=0)
    meansq = jnp.sum(summed[:, cols : cols + 3], axis=1) / width
    scale = lax.rsqrt(meansq + 1e-05)[:, None]
    total = summed[:, :cols] * scale
    grad_mine = (
        (total - next_hidden.astype(jnp.float32)) * (scale / math.sqrt(row_count))
    ).astype(jnp.bfloat16)
    grad_out = gather(grad_mine, "tp").reshape(row_count, cols)
    prediction = total.astype(jnp.bfloat16)
    weight_grad = lax.dot_general(
        all_raw, grad_out, (((0,), (0,)), ((), ())), preferred_element_type=jnp.float32
    )
    return (prediction, weight_grad.astype(jnp.bfloat16))


def solution(mesh):
    in_specs = (
        P("grp", None, "tp"),
        P("grp", None, None),
        P("grp", None, None),
        P("grp", None, "tp", None),
        P("grp", None, "tp", None),
        P("grp"),
        P("tp"),
        P("tp", "grp"),
        P("tp", "grp"),
    )
    out_specs = (P("tp", "grp"), P("tp", "grp"))
    return jax.shard_map(
        per_device, mesh=mesh, in_specs=in_specs, out_specs=out_specs, check_vma=False
    )
```

```python
import functools
import math

import jax
import jax.numpy as jnp
from jax import lax
from jax.experimental import pallas as pl
from jax.experimental.pallas import tpu as pltpu
from jax.sharding import Mesh
from jax.sharding import PartitionSpec as P

TP = ("ch", "c")
TILE = 16


def split_pieces(x):
    a = lax.reduce_precision(x, 8, 7)
    b = lax.reduce_precision(x - a, 8, 7)
    return a, b, x - a - b


def gather(x, axis):
    n = lax.axis_size(axis)
    return lax.all_to_all(jnp.broadcast_to(x[None], (n,) + x.shape), axis, 0, 0)


def swap(x):
    return lax.ppermute(x, "c", [(0, 1), (1, 0)])


def attend_kernel(steps, meta, q_ref, ko, vo, ks, vs, new_ref, out_ref, lse_ref):
    i = pl.program_id(0)
    half = pl.num_programs(0)
    kv_heads, block, head_size = ko.shape[1:]
    q_rows = q_ref.shape[1] * q_ref.shape[3]
    length = meta[3 + meta[0] * half + i]
    scale = 1.0 / math.sqrt(head_size)

    for kref, vref, base in ((ko, vo, meta[1]), (ks, vs, meta[2])):
        for j in range(steps):
            place = length + j - base

            @pl.when((place >= 0) & (place < block))
            def _(kref=kref, vref=vref, place=place, j=j):
                start = pl.multiple_of((place // TILE) * TILE, TILE)
                hit = lax.broadcasted_iota(jnp.int32, (TILE, head_size), 0) == place - start
                for k in range(kv_heads):
                    for which, ref in ((0, kref), (1, vref)):
                        slab = ref[0, k, pl.ds(start, TILE), :].astype(jnp.float32)
                        fresh = new_ref[0, which, k, j : j + 1, :]
                        ref[0, k, pl.ds(start, TILE), :] = jnp.where(hit, fresh, slab).astype(
                            jnp.bfloat16
                        )

    row = lax.broadcasted_iota(jnp.int32, (q_rows, block), 0)
    lane = lax.broadcasted_iota(jnp.int32, (q_rows, block), 1)
    limit = length + lax.rem(row, steps) + 1
    valid_o = lane + meta[1] < limit
    valid_s = lane + meta[2] < limit
    column = lax.broadcasted_iota(jnp.int32, (q_rows, 128), 1) == i
    nt = (((1,), (1,)), ((), ()))

    @pl.when(i == 0)
    def _():
        lse_ref[...] = jnp.zeros_like(lse_ref)

    for k in range(kv_heads):
        q = q_ref[k, :, 0].reshape(q_rows, head_size)
        so = lax.dot_general(q, ko[0, k], nt, preferred_element_type=jnp.float32)
        ss = lax.dot_general(q, ks[0, k], nt, preferred_element_type=jnp.float32)
        so = jnp.where(valid_o, so * scale, -1e30)
        ss = jnp.where(valid_s, ss * scale, -1e30)
        top = jnp.max(jnp.maximum(so, ss), axis=1, keepdims=True)
        po = jnp.exp(so - top)
        ps = jnp.exp(ss - top)
        total = jnp.sum(po + ps, axis=1, keepdims=True)
        acc = jnp.dot(po.astype(jnp.bfloat16), vo[0, k], preferred_element_type=jnp.float32)
        acc += jnp.dot(ps.astype(jnp.bfloat16), vs[0, k], preferred_element_type=jnp.float32)
        out_ref[k, pl.ds(pl.multiple_of(i * q_rows, q_rows), q_rows), :] = (acc / total).astype(
            jnp.bfloat16
        )
        lse = jnp.where(top > -1e29, top + jnp.log(total), -1e30)
        lse_ref[k, :q_rows, :] = jnp.where(column, lse, lse_ref[k, :q_rows, :])

    @pl.when(i == half - 1)
    def _():
        for k in range(kv_heads):
            x = lse_ref[k].T[:half]
            a = x.astype(jnp.bfloat16).astype(jnp.float32)
            b = (x - a).astype(jnp.bfloat16).astype(jnp.float32)
            c = x - a - b
            rows = jnp.concatenate([a, b, c, jnp.zeros((TILE - 3 * half, 128), jnp.float32)], 0)
            out_ref[k, half * q_rows :, :] = rows.astype(jnp.bfloat16)


def attend(steps, meta, heads, own_k, own_v, sib_k, sib_v, fresh):
    kv_heads, share, half, rows, head_size = heads.shape
    block = own_k.shape[2]
    q_rows = share * rows
    out_rows = half * q_rows + TILE
    own = pl.BlockSpec((1, kv_heads, block, head_size), lambda i, m: (m[0] * half + i, 0, 0, 0))
    sib = pl.BlockSpec((1, kv_heads, block, head_size), lambda i, m: (i, 0, 0, 0))
    return pl.pallas_call(
        functools.partial(attend_kernel, steps),
        grid_spec=pltpu.PrefetchScalarGridSpec(
            num_scalar_prefetch=1,
            grid=(half,),
            in_specs=[
                pl.BlockSpec(
                    (kv_heads, share, 1, rows, head_size), lambda i, m: (0, 0, i, 0, 0)
                ),
                own,
                own,
                sib,
                sib,
                pl.BlockSpec(
                    (1, 2, kv_heads, steps, head_size), lambda i, m: (m[0] * half + i, 0, 0, 0, 0)
                ),
            ],
            out_specs=pl.BlockSpec((kv_heads, out_rows, head_size), lambda i, m: (0, 0, 0)),
            scratch_shapes=[pltpu.VMEM((kv_heads, 128, 128), jnp.float32)],
        ),
        out_shape=jax.ShapeDtypeStruct((kv_heads, out_rows, head_size), jnp.bfloat16),
        compiler_params=pltpu.CompilerParams(
            dimension_semantics=("arbitrary",), vmem_limit_bytes=32 * 1024 * 1024
        ),
        cost_estimate=pl.CostEstimate(
            flops=half * kv_heads * q_rows * 2 * block * head_size * 4,
            bytes_accessed=half * kv_heads * block * head_size * 8,
            transcendentals=half * kv_heads * q_rows * 2 * block,
        ),
        name="attend",
    )(meta, heads, own_k, own_v, sib_k, sib_v, fresh)


def per_device(
    queries,
    new_keys,
    new_values,
    cache_keys,
    cache_values,
    lengths,
    norm_gain,
    draft_weight,
    next_hidden,
):
    chips, cores = lax.axis_size("ch"), lax.axis_size("c")
    chip, core = lax.axis_index("ch"), lax.axis_index("c")
    zh, ny = lax.axis_size("zh"), lax.axis_size("y")
    seqs, steps, feats = queries.shape
    kv_heads, block, head_size = (cache_keys.shape[1], cache_keys.shape[2], cache_keys.shape[3])
    mine = feats // head_size
    width = feats * chips * cores
    half = seqs // cores
    hrows = half * steps
    cols = draft_weight.shape[1]
    other = 1 - core

    packed = queries.reshape(cores, half, steps, mine, head_size).transpose(0, 1, 3, 2, 4)
    packed = packed.reshape(cores, half, mine * steps, head_size)
    spread = jnp.broadcast_to(packed[None], (chips,) + packed.shape)
    spread = spread.reshape((chips * cores,) + packed.shape[1:])

    sib_k = swap(lax.dynamic_slice_in_dim(cache_keys, other * half, half, 0))
    sib_v = swap(lax.dynamic_slice_in_dim(cache_values, other * half, half, 0))
    sib_w = swap(draft_weight)
    sib_gain = swap(norm_gain)
    sib_hidden = swap(lax.dynamic_slice_in_dim(next_hidden, other * hrows, hrows, 0))
    own_hidden = lax.dynamic_slice_in_dim(next_hidden, core * hrows, hrows, 0)

    heads = lax.all_to_all(spread, TP, 0, 0).reshape(
        kv_heads, cores, half, mine * steps, head_size
    )
    place = (chip * cores + core) * block
    sib_place = (chip * cores + other) * block
    meta = jnp.concatenate([jnp.stack([core, place, sib_place]).astype(jnp.int32), lengths])
    fresh = jnp.stack([new_keys, new_values], axis=1).reshape(
        seqs, 2, steps, kv_heads, head_size
    )
    fresh = fresh.transpose(0, 1, 3, 2, 4).astype(jnp.float32)
    sent = attend(steps, meta, heads, cache_keys, cache_values, sib_k, sib_v, fresh)

    got = lax.all_to_all(sent, "ch", 0, 0)
    q_rows = cores * mine * steps
    outs = got[:, : half * q_rows].astype(jnp.float32).reshape(chips, half, q_rows, head_size)
    lse = got[:, half * q_rows : half * q_rows + 3 * half, :q_rows].astype(jnp.float32)
    lse = jnp.sum(lse.reshape(chips, 3, half, q_rows), axis=1)
    factor = jnp.exp(lse - jnp.max(lse, axis=0, keepdims=True))
    context = jnp.sum(outs * factor[..., None], axis=0) / jnp.sum(factor, axis=0)[..., None]
    context = context.reshape(half, cores, mine, steps, head_size).transpose(1, 0, 3, 2, 4)
    context = context.reshape(cores, hrows, feats)
    flat_own = lax.dynamic_index_in_dim(context, core, 0, keepdims=False)
    flat_sib = lax.dynamic_index_in_dim(context, other, 0, keepdims=False)
    raw = jnp.stack([flat_own * norm_gain[None, :], flat_sib * sib_gain[None, :]])
    raw = raw.astype(jnp.bfloat16)

    by_zh = gather(raw, "zh")
    by_y = gather(by_zh, "y")
    by_y = by_y.transpose(2, 1, 0, 3, 4).reshape(2, zh * ny * hrows, feats)
    own_raw, sib_raw = by_y[0], by_y[1]
    row_half = zh * ny * hrows
    row_count = row_half * cores

    def squares(x, gain):
        plain = x.astype(jnp.float32) * (1.0 / gain)[None, :]
        return jnp.sum(plain * plain, axis=1)

    sq = squares(own_raw, norm_gain) + squares(sib_raw, sib_gain)
    sq = jnp.stack(split_pieces(sq), axis=-1).astype(jnp.bfloat16)
    sq = jnp.pad(sq, ((0, 0), (0, 128 - 3))).reshape(chips, cores * hrows, 128)
    partial = jnp.dot(own_raw, draft_weight, preferred_element_type=jnp.float32)
    partial += jnp.dot(sib_raw, sib_w, preferred_element_type=jnp.float32)
    partial = partial.astype(jnp.bfloat16).reshape(chips, cores * hrows, cols)
    oth_raw = swap(sib_raw)
    parts = lax.all_to_all(jnp.concatenate([partial, sq], axis=2), "ch", 0, 0)
    summed = jnp.sum(parts.astype(jnp.float32), axis=0)
    meansq = jnp.sum(summed[:, cols : cols + 3], axis=1) / width
    scale = lax.rsqrt(meansq + 1e-05)[:, None]
    total = summed[:, :cols] * scale

    flip = core == 1
    hid0 = jnp.where(flip, sib_hidden, own_hidden)
    hid1 = jnp.where(flip, own_hidden, sib_hidden)
    hidden = jnp.concatenate([hid0, hid1]).astype(jnp.float32)
    grad_mine = ((total - hidden) * (scale / math.sqrt(row_count))).astype(jnp.bfloat16)
    grad_half = gather(grad_mine, "ch").reshape(row_half, cols)
    grad_other = swap(grad_half)

    pred = total.astype(jnp.bfloat16).reshape(cores, hrows, cols)
    keep = jnp.where(flip, pred[1], pred[0])
    came = swap(jnp.where(flip, pred[0], pred[1]))
    prediction = jnp.concatenate([jnp.where(flip, came, keep), jnp.where(flip, keep, came)])

    tn = (((0,), (0,)), ((), ()))
    weight_grad = lax.dot_general(own_raw, grad_half, tn, preferred_element_type=jnp.float32)
    weight_grad += lax.dot_general(oth_raw, grad_other, tn, preferred_element_type=jnp.float32)
    return (prediction, weight_grad.astype(jnp.bfloat16))


def solution(mesh):
    tp, grp = mesh.devices.shape
    fine = Mesh(mesh.devices.reshape(tp // 2, 2, 4, grp // 4), ("ch", "c", "zh", "y"))
    g = ("zh", "y")
    in_specs = (
        P(g, None, TP),
        P(g, None, None),
        P(g, None, None),
        P(g, None, TP, None),
        P(g, None, TP, None),
        P(g),
        P(TP),
        P(TP, g),
        P(TP, g),
    )
    out_specs = (P(TP, g), P(TP, g))
    return jax.shard_map(
        per_device, mesh=fine, in_specs=in_specs, out_specs=out_specs, check_vma=False
    )
```

```python
import functools
import math

import jax
import jax.numpy as jnp
from jax import lax
from jax.experimental import pallas as pl
from jax.experimental.pallas import tpu as pltpu
from jax.sharding import Mesh
from jax.sharding import PartitionSpec as P

TP = ("ch", "c")
TILE = 16


def gather(x, axis):
    n = lax.axis_size(axis)
    return lax.all_to_all(jnp.broadcast_to(x[None], (n,) + x.shape), axis, 0, 0)


def shift(x, axis, k):
    n = lax.axis_size(axis)
    return lax.ppermute(x, axis, [(j, (j + k) % n) for j in range(n)])


def swap(x):
    return lax.ppermute(x, "c", [(0, 1), (1, 0)])


def attend_kernel(steps, meta, q_ref, ko, vo, ks, vs, new_ref, out_ref, buf, lse_ref, sems):
    half = buf.shape[1]
    kv_heads, block, head_size = buf.shape[2:]
    q_rows = q_ref.shape[1] * q_ref.shape[3]
    scale = math.log2(math.e) / math.sqrt(head_size)
    core = meta[0]

    def copies(i):
        out = []
        for n, ref in enumerate((ko, ks, vo, vs)):
            src = ref.at[core * half + i]
            out.append(pltpu.make_async_copy(src, buf.at[n, i], sems.at[n, i]))
        return out

    for i in range(half):
        for copy in copies(i):
            copy.start()

    row = lax.broadcasted_iota(jnp.int32, (q_rows, block), 0)
    lane = lax.broadcasted_iota(jnp.int32, (q_rows, block), 1)
    step_of = lax.rem(row, steps) + 1
    column = lax.broadcasted_iota(jnp.int32, (q_rows, 128), 1)
    nt = (((1,), (1,)), ((), ()))
    lse_ref[...] = jnp.zeros_like(lse_ref)

    def one(i):
        length = meta[3 + core * half + i]
        c = copies(i)

        def insert(n, base):
            for j in range(steps):
                place = length + j - base

                @pl.when((place >= 0) & (place < block))
                def _(place=place, j=j):
                    start = pl.multiple_of((place // TILE) * TILE, TILE)
                    hit = lax.broadcasted_iota(jnp.int32, (TILE, head_size), 0) == place - start
                    for k in range(kv_heads):
                        slab = buf[n, i, k, pl.ds(start, TILE), :].astype(jnp.float32)
                        fresh = new_ref[core * half + i, n // 2, k, j : j + 1, :]
                        buf[n, i, k, pl.ds(start, TILE), :] = jnp.where(hit, fresh, slab).astype(
                            jnp.bfloat16
                        )

        c[0].wait()
        c[1].wait()
        insert(0, meta[1])
        insert(1, meta[2])
        limit = length + step_of
        valid_o = lane + meta[1] < limit
        valid_s = lane + meta[2] < limit
        qk = []
        for k in range(kv_heads):
            q = q_ref[k, :, i].reshape(q_rows, head_size)
            so = lax.dot_general(q, buf[0, i, k], nt, preferred_element_type=jnp.float32)
            ss = lax.dot_general(q, buf[1, i, k], nt, preferred_element_type=jnp.float32)
            qk.append((so, ss))
        pr = []
        for k in range(kv_heads):
            so, ss = qk[k]
            so = jnp.where(valid_o, so * scale, -1e30)
            ss = jnp.where(valid_s, ss * scale, -1e30)
            top = jnp.max(jnp.maximum(so, ss), axis=1, keepdims=True)
            po = jnp.exp2(so - top)
            ps = jnp.exp2(ss - top)
            total = jnp.sum(po + ps, axis=1, keepdims=True)
            pr.append((top, total, po.astype(jnp.bfloat16), ps.astype(jnp.bfloat16)))
        c[2].wait()
        c[3].wait()
        insert(2, meta[1])
        insert(3, meta[2])
        for k in range(kv_heads):
            top, total, po, ps = pr[k]
            acc = jnp.dot(po, buf[2, i, k], preferred_element_type=jnp.float32)
            acc += jnp.dot(ps, buf[3, i, k], preferred_element_type=jnp.float32)
            out_ref[k, i * q_rows : (i + 1) * q_rows, :] = (acc / total).astype(jnp.bfloat16)
            lse = jnp.where(top > -1e29, top + jnp.log2(total), -1e30)
            lse_ref[k, :q_rows, :] = jnp.where(column == i, lse, lse_ref[k, :q_rows, :])

    for i in range(half):
        one(i)

    for k in range(kv_heads):
        x = lse_ref[k].T[:half]
        a = x.astype(jnp.bfloat16).astype(jnp.float32)
        b = (x - a).astype(jnp.bfloat16).astype(jnp.float32)
        c = x - a - b
        rows = jnp.concatenate([a, b, c, jnp.zeros((TILE - 3 * half, 128), jnp.float32)], 0)
        out_ref[k, half * q_rows :, :] = rows.astype(jnp.bfloat16)


def attend(steps, meta, heads, own_k, own_v, sib_k, sib_v, fresh):
    kv_heads, share, half, rows, head_size = heads.shape
    block = own_k.shape[2]
    q_rows = share * rows
    out_rows = half * q_rows + TILE
    vmem = pl.BlockSpec(memory_space=pltpu.VMEM)
    hbm = pl.BlockSpec(memory_space=pl.ANY)
    return pl.pallas_call(
        functools.partial(attend_kernel, steps),
        in_specs=[pl.BlockSpec(memory_space=pltpu.SMEM), vmem, hbm, hbm, hbm, hbm, vmem],
        out_specs=vmem,
        scratch_shapes=[
            pltpu.VMEM((4, half, kv_heads, block, head_size), jnp.bfloat16),
            pltpu.VMEM((kv_heads, 128, 128), jnp.float32),
            pltpu.SemaphoreType.DMA((4, half)),
        ],
        out_shape=jax.ShapeDtypeStruct((kv_heads, out_rows, head_size), jnp.bfloat16),
        compiler_params=pltpu.CompilerParams(vmem_limit_bytes=60 * 1024 * 1024),
        cost_estimate=pl.CostEstimate(
            flops=half * kv_heads * q_rows * 2 * block * head_size * 4,
            bytes_accessed=half * kv_heads * block * head_size * 8,
            transcendentals=half * kv_heads * q_rows * 2 * block,
        ),
        name="attend",
    )(meta, heads, own_k, own_v, sib_k, sib_v, fresh)


def project_kernel(place, *refs):
    blocks, (g_own, g_sib, w_own, w_sib, out_ref, own_ref, sib_ref) = refs[:-7], refs[-7:]
    hrows = blocks[0].shape[2]
    tile = w_own.shape[1]
    cols = tile * pl.num_programs(0)
    t = pl.program_id(0)

    @pl.when(t == 0)
    def _():
        for n, ref in enumerate(blocks):
            y_back, z_backs = n // 2, ((0, 1, 3), (2,))[n % 2]
            y = lax.rem(place[1] - y_back + 4, 4)
            for at, z_back in enumerate(z_backs):
                z = lax.rem(place[0] - z_back + 4, 4)
                rows = pl.ds(pl.multiple_of((z * 4 + y) * hrows, hrows), hrows)
                own_ref[rows, :] = ref[at, 0]
                sib_ref[rows, :] = ref[at, 1]
        own = own_ref[...].astype(jnp.float32) * (1.0 / g_own[...])
        sib = sib_ref[...].astype(jnp.float32) * (1.0 / g_sib[...])
        sq = jnp.sum(own * own + sib * sib, axis=1, keepdims=True)
        a = sq.astype(jnp.bfloat16).astype(jnp.float32)
        b = (sq - a).astype(jnp.bfloat16).astype(jnp.float32)
        lane = lax.broadcasted_iota(jnp.int32, (sq.shape[0], 128), 1)
        pieces = jnp.where(lane == 0, a, jnp.where(lane == 1, b, sq - a - b))
        out_ref[:, cols:] = jnp.where(lane < 3, pieces, 0.0).astype(jnp.bfloat16)

    acc = jnp.dot(own_ref[...], w_own[...], preferred_element_type=jnp.float32)
    acc += jnp.dot(sib_ref[...], w_sib[...], preferred_element_type=jnp.float32)
    out_ref[:, pl.ds(pl.multiple_of(t * tile, tile), tile)] = acc.astype(jnp.bfloat16)


def project(place, blocks, g_own, g_sib, w_own, w_sib):
    hrows, feats = blocks[0].shape[2:]
    cols = w_own.shape[1]
    rows = 16 * hrows
    tile = 256
    whole = lambda x: pl.BlockSpec(x.shape, lambda t, m, n=len(x.shape): (0,) * n)
    weights = pl.BlockSpec((feats, tile), lambda t, m: (0, t))
    outs = (
        jax.ShapeDtypeStruct((rows, cols + 128), jnp.bfloat16),
        jax.ShapeDtypeStruct((rows, feats), jnp.bfloat16),
        jax.ShapeDtypeStruct((rows, feats), jnp.bfloat16),
    )
    return pl.pallas_call(
        project_kernel,
        grid_spec=pltpu.PrefetchScalarGridSpec(
            num_scalar_prefetch=1,
            grid=(cols // tile,),
            in_specs=[whole(x) for x in blocks] + [whole(g_own), whole(g_sib), weights, weights],
            out_specs=tuple(whole(x) for x in outs),
        ),
        out_shape=outs,
        compiler_params=pltpu.CompilerParams(
            dimension_semantics=("arbitrary",), vmem_limit_bytes=40 * 1024 * 1024
        ),
        cost_estimate=pl.CostEstimate(
            flops=rows * feats * cols * 4, bytes_accessed=feats * cols * 4, transcendentals=0
        ),
        name="project",
    )(place, *blocks, g_own, g_sib, w_own, w_sib)


def per_device(
    queries,
    new_keys,
    new_values,
    cache_keys,
    cache_values,
    lengths,
    norm_gain,
    draft_weight,
    next_hidden,
):
    chips, cores = lax.axis_size("ch"), lax.axis_size("c")
    chip, core = lax.axis_index("ch"), lax.axis_index("c")
    zh, ny = lax.axis_size("zh"), lax.axis_size("y")
    seqs, steps, feats = queries.shape
    kv_heads, block, head_size = (cache_keys.shape[1], cache_keys.shape[2], cache_keys.shape[3])
    mine = feats // head_size
    width = feats * chips * cores
    half = seqs // cores
    hrows = half * steps
    cols = draft_weight.shape[1]
    other = 1 - core

    packed = queries.reshape(cores, half, steps, mine, head_size).transpose(0, 1, 3, 2, 4)
    packed = packed.reshape(cores, half, mine * steps, head_size)
    spread = jnp.broadcast_to(packed[None], (chips,) + packed.shape)
    spread = spread.reshape((chips * cores,) + packed.shape[1:])

    sib_k = swap(cache_keys)
    sib_v = swap(cache_values)
    sib_w = swap(draft_weight)
    sib_gain = swap(norm_gain)
    sib_hidden = swap(lax.dynamic_slice_in_dim(next_hidden, other * hrows, hrows, 0))
    own_hidden = lax.dynamic_slice_in_dim(next_hidden, core * hrows, hrows, 0)

    heads = lax.all_to_all(spread, TP, 0, 0).reshape(
        kv_heads, cores, half, mine * steps, head_size
    )
    place = (chip * cores + core) * block
    sib_place = (chip * cores + other) * block
    meta = jnp.concatenate([jnp.stack([core, place, sib_place]).astype(jnp.int32), lengths])
    fresh = jnp.stack([new_keys, new_values], axis=1).reshape(
        seqs, 2, steps, kv_heads, head_size
    )
    fresh = fresh.transpose(0, 1, 3, 2, 4).astype(jnp.float32)
    sent = attend(steps, meta, heads, cache_keys, cache_values, sib_k, sib_v, fresh)

    got = lax.all_to_all(sent, "ch", 0, 0)
    q_rows = cores * mine * steps
    outs = got[:, : half * q_rows].astype(jnp.float32).reshape(chips, half, q_rows, head_size)
    lse = got[:, half * q_rows : half * q_rows + 3 * half, :q_rows].astype(jnp.float32)
    lse = jnp.sum(lse.reshape(chips, 3, half, q_rows), axis=1)
    factor = jnp.exp2(lse - jnp.max(lse, axis=0, keepdims=True))
    context = jnp.sum(outs * factor[..., None], axis=0) / jnp.sum(factor, axis=0)[..., None]
    context = context.reshape(half, cores, mine, steps, head_size).transpose(1, 0, 3, 2, 4)
    context = context.reshape(cores, hrows, feats)
    flat_own = lax.dynamic_index_in_dim(context, core, 0, keepdims=False)
    flat_sib = lax.dynamic_index_in_dim(context, other, 0, keepdims=False)
    raw = jnp.stack([flat_own * norm_gain[None, :], flat_sib * sib_gain[None, :]])
    raw = raw.astype(jnp.bfloat16)

    near = jnp.stack([raw, shift(raw, "zh", 1), shift(raw, "zh", 3)])
    far = shift(raw, "zh", 2)[None]
    blocks = [near, far]
    for k in (1, 2, 3):
        blocks += [shift(near, "y", k), shift(far, "y", k)]
    row_half = zh * ny * hrows
    row_count = row_half * cores
    where = jnp.stack([lax.axis_index("zh"), lax.axis_index("y")]).astype(jnp.int32)
    partial, own_raw, sib_raw = project(
        where, blocks, norm_gain[None, :], sib_gain[None, :], draft_weight, sib_w
    )
    payload = partial.reshape(chips, cores * hrows, cols + 128)
    oth_raw = swap(sib_raw)
    parts = lax.all_to_all(payload, "ch", 0, 0)
    summed = jnp.sum(parts.astype(jnp.float32), axis=0)
    meansq = jnp.sum(summed[:, cols : cols + 3], axis=1) / width
    scale = lax.rsqrt(meansq + 1e-05)[:, None]
    total = summed[:, :cols] * scale

    flip = core == 1
    hid0 = jnp.where(flip, sib_hidden, own_hidden)
    hid1 = jnp.where(flip, own_hidden, sib_hidden)
    hidden = jnp.concatenate([hid0, hid1]).astype(jnp.float32)
    grad_mine = ((total - hidden) * (scale / math.sqrt(row_count))).astype(jnp.bfloat16)
    grad_half = gather(grad_mine, "ch").reshape(row_half, cols)
    grad_other = swap(grad_half)

    pred = total.astype(jnp.bfloat16).reshape(cores, hrows, cols)
    keep = jnp.where(flip, pred[1], pred[0])
    came = swap(jnp.where(flip, pred[0], pred[1]))
    prediction = jnp.concatenate([jnp.where(flip, came, keep), jnp.where(flip, keep, came)])

    tn = (((0,), (0,)), ((), ()))
    weight_grad = lax.dot_general(own_raw, grad_half, tn, preferred_element_type=jnp.float32)
    weight_grad += lax.dot_general(oth_raw, grad_other, tn, preferred_element_type=jnp.float32)
    return (prediction, weight_grad.astype(jnp.bfloat16))


def solution(mesh):
    tp, grp = mesh.devices.shape
    fine = Mesh(mesh.devices.reshape(tp // 2, 2, 4, grp // 4), ("ch", "c", "zh", "y"))
    g = ("zh", "y")
    in_specs = (
        P(g, None, TP),
        P(g, None, None),
        P(g, None, None),
        P(g, None, TP, None),
        P(g, None, TP, None),
        P(g),
        P(TP),
        P(TP, g),
        P(TP, g),
    )
    out_specs = (P(TP, g), P(TP, g))
    return jax.shard_map(
        per_device, mesh=fine, in_specs=in_specs, out_specs=out_specs, check_vma=False
    )
```

```python
import functools
import math

import jax
import jax.numpy as jnp
from jax import lax
from jax.experimental import pallas as pl
from jax.experimental.pallas import tpu as pltpu
from jax.sharding import Mesh
from jax.sharding import PartitionSpec as P

TP = ("ch", "c")
TILE = 16


def gather(x, axis):
    n = lax.axis_size(axis)
    return lax.all_to_all(jnp.broadcast_to(x[None], (n,) + x.shape), axis, 0, 0)


def in_hbm(x):
    return pltpu.with_memory_space_constraint(x, pltpu.HBM)


def in_vmem(x):
    return pltpu.with_memory_space_constraint(x, pltpu.VMEM)


def shift(x, axis, k):
    n = lax.axis_size(axis)
    return lax.ppermute(x, axis, [(j, (j + k) % n) for j in range(n)])


def swap(x):
    return lax.ppermute(x, "c", [(0, 1), (1, 0)])


def attend_kernel(steps, meta, q_ref, ko, vo, ks, vs, new_ref, out_ref, buf, lse_ref, sems):
    half = buf.shape[1]
    kv_heads, block, head_size = buf.shape[2:]
    q_rows = q_ref.shape[1] * q_ref.shape[3]
    scale = math.log2(math.e) / math.sqrt(head_size)
    core = meta[0]

    def copies(i):
        out = []
        for n, ref in enumerate((ko, ks, vo, vs)):
            src = ref.at[core * half + i]
            out.append(pltpu.make_async_copy(src, buf.at[n, i], sems.at[n, i]))
        return out

    for i in range(half):
        for copy in copies(i):
            copy.start()

    row = lax.broadcasted_iota(jnp.int32, (q_rows, block), 0)
    lane = lax.broadcasted_iota(jnp.int32, (q_rows, block), 1)
    step_of = lax.rem(row, steps) + 1
    column = lax.broadcasted_iota(jnp.int32, (q_rows, 128), 1)
    nt = (((1,), (1,)), ((), ()))
    lse_ref[...] = jnp.zeros_like(lse_ref)

    def one(i):
        length = meta[3 + core * half + i]
        c = copies(i)

        def insert(n, base):
            for j in range(steps):
                place = length + j - base

                @pl.when((place >= 0) & (place < block))
                def _(place=place, j=j):
                    start = pl.multiple_of((place // TILE) * TILE, TILE)
                    hit = lax.broadcasted_iota(jnp.int32, (TILE, head_size), 0) == place - start
                    for k in range(kv_heads):
                        slab = buf[n, i, k, pl.ds(start, TILE), :].astype(jnp.float32)
                        fresh = new_ref[core * half + i, n // 2, k, j : j + 1, :]
                        buf[n, i, k, pl.ds(start, TILE), :] = jnp.where(hit, fresh, slab).astype(
                            jnp.bfloat16
                        )

        c[0].wait()
        c[1].wait()
        insert(0, meta[1])
        insert(1, meta[2])
        limit = length + step_of
        valid_o = lane + meta[1] < limit
        valid_s = lane + meta[2] < limit
        qk = []
        for k in range(kv_heads):
            q = q_ref[k, :, i].reshape(q_rows, head_size)
            so = lax.dot_general(q, buf[0, i, k], nt, preferred_element_type=jnp.float32)
            ss = lax.dot_general(q, buf[1, i, k], nt, preferred_element_type=jnp.float32)
            qk.append((so, ss))
        pr = []
        for k in range(kv_heads):
            so, ss = qk[k]
            so = jnp.where(valid_o, so * scale, -1e30)
            ss = jnp.where(valid_s, ss * scale, -1e30)
            top = jnp.max(jnp.maximum(so, ss), axis=1, keepdims=True)
            po = jnp.exp2(so - top)
            ps = jnp.exp2(ss - top)
            total = jnp.sum(po + ps, axis=1, keepdims=True)
            pr.append((top, total, po.astype(jnp.bfloat16), ps.astype(jnp.bfloat16)))
        c[2].wait()
        c[3].wait()
        insert(2, meta[1])
        insert(3, meta[2])
        for k in range(kv_heads):
            top, total, po, ps = pr[k]
            acc = jnp.dot(po, buf[2, i, k], preferred_element_type=jnp.float32)
            acc += jnp.dot(ps, buf[3, i, k], preferred_element_type=jnp.float32)
            out_ref[k, i * q_rows : (i + 1) * q_rows, :] = (acc / total).astype(jnp.bfloat16)
            lse = jnp.where(top > -1e29, top + jnp.log2(total), -1e30)
            lse_ref[k, :q_rows, :] = jnp.where(column == i, lse, lse_ref[k, :q_rows, :])

    for i in range(half):
        one(i)

    for k in range(kv_heads):
        x = lse_ref[k].T[:half]
        a = x.astype(jnp.bfloat16).astype(jnp.float32)
        b = (x - a).astype(jnp.bfloat16).astype(jnp.float32)
        c = x - a - b
        rows = jnp.concatenate([a, b, c, jnp.zeros((TILE - 3 * half, 128), jnp.float32)], 0)
        out_ref[k, half * q_rows :, :] = rows.astype(jnp.bfloat16)


def attend(steps, meta, heads, own_k, own_v, sib_k, sib_v, fresh):
    kv_heads, share, half, rows, head_size = heads.shape
    block = own_k.shape[2]
    q_rows = share * rows
    out_rows = half * q_rows + TILE
    vmem = pl.BlockSpec(memory_space=pltpu.VMEM)
    hbm = pl.BlockSpec(memory_space=pl.ANY)
    return pl.pallas_call(
        functools.partial(attend_kernel, steps),
        in_specs=[pl.BlockSpec(memory_space=pltpu.SMEM), vmem, hbm, hbm, hbm, hbm, vmem],
        out_specs=vmem,
        scratch_shapes=[
            pltpu.VMEM((4, half, kv_heads, block, head_size), jnp.bfloat16),
            pltpu.VMEM((kv_heads, 128, 128), jnp.float32),
            pltpu.SemaphoreType.DMA((4, half)),
        ],
        out_shape=jax.ShapeDtypeStruct((kv_heads, out_rows, head_size), jnp.bfloat16),
        compiler_params=pltpu.CompilerParams(vmem_limit_bytes=28 * 1024 * 1024),
        cost_estimate=pl.CostEstimate(
            flops=half * kv_heads * q_rows * 2 * block * head_size * 4,
            bytes_accessed=half * kv_heads * block * head_size * 8,
            transcendentals=half * kv_heads * q_rows * 2 * block,
        ),
        name="attend",
    )(meta, heads, *map(in_hbm, (own_k, own_v, sib_k, sib_v)), fresh)


def project_kernel(tile, place, *refs):
    blocks, refs = refs[:-10], refs[-10:]
    g_own, g_sib, w_own, w_sib, out_ref, own_out, sib_out, own_ref, sib_ref, sems = refs
    hrows = blocks[0].shape[2]
    feats, cols = w_own.shape
    for n, ref in enumerate(blocks):
        y_back, z_backs = n // 2, ((0, 1, 3), (2,))[n % 2]
        y = lax.rem(place[1] - y_back + 4, 4)
        for at, z_back in enumerate(z_backs):
            z = lax.rem(place[0] - z_back + 4, 4)
            rows = pl.ds(pl.multiple_of((z * 4 + y) * hrows, hrows), hrows)
            own_ref[rows, :] = ref[at, 0]
            sib_ref[rows, :] = ref[at, 1]
    copies = [
        pltpu.make_async_copy(own_ref, own_out, sems.at[0]),
        pltpu.make_async_copy(sib_ref, sib_out, sems.at[1]),
    ]
    for copy in copies:
        copy.start()
    own, sib = own_ref[...], sib_ref[...]
    for t in range(0, cols, tile):
        acc = jnp.dot(own, w_own[:, t : t + tile], preferred_element_type=jnp.float32)
        acc += jnp.dot(sib, w_sib[:, t : t + tile], preferred_element_type=jnp.float32)
        out_ref[:, t : t + tile] = acc.astype(jnp.bfloat16)
    sq = 0.0
    for t in range(0, feats, 128):
        a = own_ref[:, t : t + 128].astype(jnp.float32) * (1.0 / g_own[:, t : t + 128])
        b = sib_ref[:, t : t + 128].astype(jnp.float32) * (1.0 / g_sib[:, t : t + 128])
        sq = sq + a * a + b * b
    sq = jnp.sum(sq, axis=1, keepdims=True)
    a = sq.astype(jnp.bfloat16).astype(jnp.float32)
    b = (sq - a).astype(jnp.bfloat16).astype(jnp.float32)
    lane = lax.broadcasted_iota(jnp.int32, (sq.shape[0], 128), 1)
    pieces = jnp.where(lane == 0, a, jnp.where(lane == 1, b, sq - a - b))
    out_ref[:, cols:] = jnp.where(lane < 3, pieces, 0.0).astype(jnp.bfloat16)
    for copy in copies:
        copy.wait()


def project(place, blocks, g_own, g_sib, w_own, w_sib):
    hrows, feats = blocks[0].shape[2:]
    cols = w_own.shape[1]
    rows = 16 * hrows
    vmem = pl.BlockSpec(memory_space=pltpu.VMEM)
    hbm = pl.BlockSpec(memory_space=pl.ANY)
    outs = (
        jax.ShapeDtypeStruct((rows, cols + 128), jnp.bfloat16),
        pltpu.HBM((rows, feats), jnp.bfloat16),
        pltpu.HBM((rows, feats), jnp.bfloat16),
    )
    return pl.pallas_call(
        functools.partial(project_kernel, 256),
        in_specs=[pl.BlockSpec(memory_space=pltpu.SMEM)] + [vmem] * (len(blocks) + 4),
        out_specs=(vmem, hbm, hbm),
        scratch_shapes=[
            pltpu.VMEM((rows, feats), jnp.bfloat16),
            pltpu.VMEM((rows, feats), jnp.bfloat16),
            pltpu.SemaphoreType.DMA((2,)),
        ],
        out_shape=outs,
        compiler_params=pltpu.CompilerParams(vmem_limit_bytes=24 * 1024 * 1024),
        cost_estimate=pl.CostEstimate(
            flops=rows * feats * cols * 4, bytes_accessed=feats * cols * 4, transcendentals=0
        ),
        name="project",
    )(place, *map(in_vmem, blocks), g_own, g_sib, in_vmem(w_own), in_vmem(w_sib))


def per_device(
    queries,
    new_keys,
    new_values,
    cache_keys,
    cache_values,
    lengths,
    norm_gain,
    draft_weight,
    next_hidden,
):
    chips, cores = lax.axis_size("ch"), lax.axis_size("c")
    chip, core = lax.axis_index("ch"), lax.axis_index("c")
    zh, ny = lax.axis_size("zh"), lax.axis_size("y")
    seqs, steps, feats = queries.shape
    kv_heads, block, head_size = (cache_keys.shape[1], cache_keys.shape[2], cache_keys.shape[3])
    mine = feats // head_size
    width = feats * chips * cores
    half = seqs // cores
    hrows = half * steps
    cols = draft_weight.shape[1]
    other = 1 - core

    packed = queries.reshape(cores, half, steps, mine, head_size).transpose(0, 1, 3, 2, 4)
    packed = packed.reshape(cores, half, mine * steps, head_size)
    spread = jnp.broadcast_to(packed[None], (chips,) + packed.shape)
    spread = spread.reshape((chips * cores,) + packed.shape[1:])

    sib_k = swap(cache_keys)
    sib_v = swap(cache_values)
    sib_w = swap(draft_weight)
    sib_gain = swap(norm_gain)
    sib_hidden = swap(lax.dynamic_slice_in_dim(next_hidden, other * hrows, hrows, 0))
    own_hidden = lax.dynamic_slice_in_dim(next_hidden, core * hrows, hrows, 0)

    heads = lax.all_to_all(spread, TP, 0, 0).reshape(
        kv_heads, cores, half, mine * steps, head_size
    )
    place = (chip * cores + core) * block
    sib_place = (chip * cores + other) * block
    meta = jnp.concatenate([jnp.stack([core, place, sib_place]).astype(jnp.int32), lengths])
    fresh = jnp.stack([new_keys, new_values], axis=1).reshape(
        seqs, 2, steps, kv_heads, head_size
    )
    fresh = fresh.transpose(0, 1, 3, 2, 4).astype(jnp.float32)
    sent = attend(steps, meta, heads, cache_keys, cache_values, sib_k, sib_v, fresh)

    got = lax.all_to_all(sent, "ch", 0, 0)
    q_rows = cores * mine * steps
    outs = got[:, : half * q_rows].astype(jnp.float32).reshape(chips, half, q_rows, head_size)
    lse = got[:, half * q_rows : half * q_rows + 3 * half, :q_rows].astype(jnp.float32)
    lse = jnp.sum(lse.reshape(chips, 3, half, q_rows), axis=1)
    factor = jnp.exp2(lse - jnp.max(lse, axis=0, keepdims=True))
    context = jnp.sum(outs * factor[..., None], axis=0) / jnp.sum(factor, axis=0)[..., None]
    context = context.reshape(half, cores, mine, steps, head_size).transpose(1, 0, 3, 2, 4)
    context = context.reshape(cores, hrows, feats)
    flat_own = lax.dynamic_index_in_dim(context, core, 0, keepdims=False)
    flat_sib = lax.dynamic_index_in_dim(context, other, 0, keepdims=False)
    raw = jnp.stack([flat_own * norm_gain[None, :], flat_sib * sib_gain[None, :]])
    raw = raw.astype(jnp.bfloat16)

    near = jnp.stack([raw, shift(raw, "zh", 1), shift(raw, "zh", 3)])
    far = shift(raw, "zh", 2)[None]
    blocks = [near, far]
    for k in (1, 2, 3):
        blocks += [shift(near, "y", k), shift(far, "y", k)]
    row_half = zh * ny * hrows
    row_count = row_half * cores
    where = jnp.stack([lax.axis_index("zh"), lax.axis_index("y")]).astype(jnp.int32)
    partial, own_raw, sib_raw = project(
        where, blocks, norm_gain[None, :], sib_gain[None, :], draft_weight, sib_w
    )
    payload = partial.reshape(chips, cores * hrows, cols + 128)
    oth_raw = swap(sib_raw)
    parts = lax.all_to_all(payload, "ch", 0, 0)
    summed = jnp.sum(parts.astype(jnp.float32), axis=0)
    meansq = jnp.sum(summed[:, cols : cols + 3], axis=1) / width
    scale = lax.rsqrt(meansq + 1e-05)[:, None]
    total = summed[:, :cols] * scale

    flip = core == 1
    hid0 = jnp.where(flip, sib_hidden, own_hidden)
    hid1 = jnp.where(flip, own_hidden, sib_hidden)
    hidden = jnp.concatenate([hid0, hid1]).astype(jnp.float32)
    grad_mine = ((total - hidden) * (scale / math.sqrt(row_count))).astype(jnp.bfloat16)
    pred = total.astype(jnp.bfloat16).reshape(cores, hrows, cols)
    keep = jnp.where(flip, pred[1], pred[0])
    came = swap(jnp.where(flip, pred[0], pred[1]))
    grad_half = gather(grad_mine, "ch").reshape(row_half, cols)
    prediction = jnp.concatenate([jnp.where(flip, came, keep), jnp.where(flip, keep, came)])
    grad_half, prediction = lax.optimization_barrier((grad_half, prediction))
    grad_other = swap(grad_half)

    tn = (((0,), (0,)), ((), ()))
    weight_grad = lax.dot_general(oth_raw, grad_other, tn, preferred_element_type=jnp.float32)
    weight_grad += lax.dot_general(own_raw, grad_half, tn, preferred_element_type=jnp.float32)
    return (prediction, weight_grad.astype(jnp.bfloat16))


def solution(mesh):
    tp, grp = mesh.devices.shape
    fine = Mesh(mesh.devices.reshape(tp // 2, 2, 4, grp // 4), ("ch", "c", "zh", "y"))
    g = ("zh", "y")
    in_specs = (
        P(g, None, TP),
        P(g, None, None),
        P(g, None, None),
        P(g, None, TP, None),
        P(g, None, TP, None),
        P(g),
        P(TP),
        P(TP, g),
        P(TP, g),
    )
    out_specs = (P(TP, g), P(TP, g))
    return jax.shard_map(
        per_device, mesh=fine, in_specs=in_specs, out_specs=out_specs, check_vma=False
    )
```

```python
import functools
import math

import jax
import jax.numpy as jnp
from jax import lax
from jax.experimental import pallas as pl
from jax.experimental.pallas import tpu as pltpu
from jax.sharding import Mesh
from jax.sharding import PartitionSpec as P

TP = ("ch", "c")
TILE = 16


def gather(x, axis):
    n = lax.axis_size(axis)
    return lax.all_to_all(jnp.broadcast_to(x[None], (n,) + x.shape), axis, 0, 0)


def in_hbm(x):
    return pltpu.with_memory_space_constraint(x, pltpu.HBM)


def in_vmem(x):
    return pltpu.with_memory_space_constraint(x, pltpu.VMEM)


def shift(x, axis, k):
    n = lax.axis_size(axis)
    return lax.ppermute(x, axis, [(j, (j + k) % n) for j in range(n)])


def swap(x):
    return lax.ppermute(x, "c", [(0, 1), (1, 0)])


def attend_kernel(steps, meta, q_ref, ko, vo, ks, vs, new_ref, out_ref, buf, lse_ref, sems):
    half = buf.shape[1]
    kv_heads, block, head_size = buf.shape[2:]
    q_rows = q_ref.shape[1] * q_ref.shape[3]
    scale = math.log2(math.e) / math.sqrt(head_size)
    core = meta[0]

    def copies(i):
        out = []
        for n, ref in enumerate((ko, ks, vo, vs)):
            src = ref.at[core * half + i]
            out.append(pltpu.make_async_copy(src, buf.at[n, i], sems.at[n, i]))
        return out

    for i in range(half):
        for copy in copies(i):
            copy.start()

    row = lax.broadcasted_iota(jnp.int32, (q_rows, block), 0)
    lane = lax.broadcasted_iota(jnp.int32, (q_rows, block), 1)
    step_of = lax.rem(row, steps) + 1
    column = lax.broadcasted_iota(jnp.int32, (q_rows, 128), 1)
    nt = (((1,), (1,)), ((), ()))
    lse_ref[...] = jnp.zeros_like(lse_ref)

    def one(i):
        length = meta[3 + core * half + i]
        c = copies(i)

        def insert(n, base):
            for j in range(steps):
                place = length + j - base

                @pl.when((place >= 0) & (place < block))
                def _(place=place, j=j):
                    start = pl.multiple_of((place // TILE) * TILE, TILE)
                    hit = lax.broadcasted_iota(jnp.int32, (TILE, head_size), 0) == place - start
                    for k in range(kv_heads):
                        slab = buf[n, i, k, pl.ds(start, TILE), :].astype(jnp.float32)
                        fresh = new_ref[core * half + i, n // 2, k, j : j + 1, :]
                        buf[n, i, k, pl.ds(start, TILE), :] = jnp.where(hit, fresh, slab).astype(
                            jnp.bfloat16
                        )

        c[0].wait()
        c[1].wait()
        insert(0, meta[1])
        insert(1, meta[2])
        limit = length + step_of
        valid_o = lane + meta[1] < limit
        valid_s = lane + meta[2] < limit
        qk = []
        for k in range(kv_heads):
            q = q_ref[k, :, i].reshape(q_rows, head_size)
            so = lax.dot_general(q, buf[0, i, k], nt, preferred_element_type=jnp.float32)
            ss = lax.dot_general(q, buf[1, i, k], nt, preferred_element_type=jnp.float32)
            qk.append((so, ss))
        pr = []
        for k in range(kv_heads):
            so, ss = qk[k]
            so = jnp.where(valid_o, so * scale, -1e30)
            ss = jnp.where(valid_s, ss * scale, -1e30)
            top = jnp.max(jnp.maximum(so, ss), axis=1, keepdims=True)
            po = jnp.exp2(so - top)
            ps = jnp.exp2(ss - top)
            total = jnp.sum(po + ps, axis=1, keepdims=True)
            pr.append((top, total, po.astype(jnp.bfloat16), ps.astype(jnp.bfloat16)))
        c[2].wait()
        c[3].wait()
        insert(2, meta[1])
        insert(3, meta[2])
        for k in range(kv_heads):
            top, total, po, ps = pr[k]
            acc = jnp.dot(po, buf[2, i, k], preferred_element_type=jnp.float32)
            acc += jnp.dot(ps, buf[3, i, k], preferred_element_type=jnp.float32)
            out_ref[k, i * q_rows : (i + 1) * q_rows, :] = (acc / total).astype(jnp.bfloat16)
            lse = jnp.where(top > -1e29, top + jnp.log2(total), -1e30)
            lse_ref[k, :q_rows, :] = jnp.where(column == i, lse, lse_ref[k, :q_rows, :])

    for i in range(half):
        one(i)

    for k in range(kv_heads):
        x = lse_ref[k].T[:half]
        a = x.astype(jnp.bfloat16).astype(jnp.float32)
        b = (x - a).astype(jnp.bfloat16).astype(jnp.float32)
        c = x - a - b
        rows = jnp.concatenate([a, b, c, jnp.zeros((TILE - 3 * half, 128), jnp.float32)], 0)
        out_ref[k, half * q_rows :, :] = rows.astype(jnp.bfloat16)


def attend(steps, meta, heads, own_k, own_v, sib_k, sib_v, fresh):
    kv_heads, share, half, rows, head_size = heads.shape
    block = own_k.shape[2]
    q_rows = share * rows
    out_rows = half * q_rows + TILE
    vmem = pl.BlockSpec(memory_space=pltpu.VMEM)
    hbm = pl.BlockSpec(memory_space=pl.ANY)
    return pl.pallas_call(
        functools.partial(attend_kernel, steps),
        in_specs=[pl.BlockSpec(memory_space=pltpu.SMEM), vmem, hbm, hbm, hbm, hbm, vmem],
        out_specs=vmem,
        scratch_shapes=[
            pltpu.VMEM((4, half, kv_heads, block, head_size), jnp.bfloat16),
            pltpu.VMEM((kv_heads, 128, 128), jnp.float32),
            pltpu.SemaphoreType.DMA((4, half)),
        ],
        out_shape=jax.ShapeDtypeStruct((kv_heads, out_rows, head_size), jnp.bfloat16),
        compiler_params=pltpu.CompilerParams(vmem_limit_bytes=28 * 1024 * 1024),
        cost_estimate=pl.CostEstimate(
            flops=half * kv_heads * q_rows * 2 * block * head_size * 4,
            bytes_accessed=half * kv_heads * block * head_size * 8,
            transcendentals=half * kv_heads * q_rows * 2 * block,
        ),
        name="attend",
    )(meta, heads, *map(in_hbm, (own_k, own_v, sib_k, sib_v)), fresh)


def project_kernel(tile, place, *refs):
    blocks, refs = refs[:-10], refs[-10:]
    g_own, g_sib, w_own, w_sib, out_ref, own_out, sib_out, own_ref, sib_ref, sems = refs
    hrows = blocks[0].shape[2]
    feats, cols = w_own.shape
    for n, ref in enumerate(blocks):
        y_back, z_backs = (0, 1, 3, 2)[n // 2], ((1, 3), (0, 2))[n % 2]
        y = lax.rem(place[1] - y_back + 4, 4)
        for at, z_back in enumerate(z_backs):
            z = lax.rem(place[0] - z_back + 4, 4)
            rows = pl.ds(pl.multiple_of((z * 4 + y) * hrows, hrows), hrows)
            own_ref[rows, :] = ref[at, 0]
            sib_ref[rows, :] = ref[at, 1]
    copies = [
        pltpu.make_async_copy(own_ref, own_out, sems.at[0]),
        pltpu.make_async_copy(sib_ref, sib_out, sems.at[1]),
    ]
    for copy in copies:
        copy.start()
    own, sib = own_ref[...], sib_ref[...]
    for t in range(0, cols, tile):
        acc = jnp.dot(own, w_own[:, t : t + tile], preferred_element_type=jnp.float32)
        acc += jnp.dot(sib, w_sib[:, t : t + tile], preferred_element_type=jnp.float32)
        out_ref[:, t : t + tile] = acc.astype(jnp.bfloat16)
    sq = 0.0
    for t in range(0, feats, 128):
        a = own_ref[:, t : t + 128].astype(jnp.float32) * (1.0 / g_own[:, t : t + 128])
        b = sib_ref[:, t : t + 128].astype(jnp.float32) * (1.0 / g_sib[:, t : t + 128])
        sq = sq + a * a + b * b
    sq = jnp.sum(sq, axis=1, keepdims=True)
    a = sq.astype(jnp.bfloat16).astype(jnp.float32)
    b = (sq - a).astype(jnp.bfloat16).astype(jnp.float32)
    lane = lax.broadcasted_iota(jnp.int32, (sq.shape[0], 128), 1)
    pieces = jnp.where(lane == 0, a, jnp.where(lane == 1, b, sq - a - b))
    out_ref[:, cols:] = jnp.where(lane < 3, pieces, 0.0).astype(jnp.bfloat16)
    for copy in copies:
        copy.wait()


def project(place, blocks, g_own, g_sib, w_own, w_sib):
    hrows, feats = blocks[0].shape[2:]
    cols = w_own.shape[1]
    rows = 16 * hrows
    vmem = pl.BlockSpec(memory_space=pltpu.VMEM)
    hbm = pl.BlockSpec(memory_space=pl.ANY)
    outs = (
        jax.ShapeDtypeStruct((rows, cols + 128), jnp.bfloat16),
        pltpu.HBM((rows, feats), jnp.bfloat16),
        pltpu.HBM((rows, feats), jnp.bfloat16),
    )
    return pl.pallas_call(
        functools.partial(project_kernel, 256),
        in_specs=[pl.BlockSpec(memory_space=pltpu.SMEM)] + [vmem] * (len(blocks) + 4),
        out_specs=(vmem, hbm, hbm),
        scratch_shapes=[
            pltpu.VMEM((rows, feats), jnp.bfloat16),
            pltpu.VMEM((rows, feats), jnp.bfloat16),
            pltpu.SemaphoreType.DMA((2,)),
        ],
        out_shape=outs,
        compiler_params=pltpu.CompilerParams(vmem_limit_bytes=24 * 1024 * 1024),
        cost_estimate=pl.CostEstimate(
            flops=rows * feats * cols * 4, bytes_accessed=feats * cols * 4, transcendentals=0
        ),
        name="project",
    )(place, *map(in_vmem, blocks), g_own, g_sib, in_vmem(w_own), in_vmem(w_sib))


def per_device(
    queries,
    new_keys,
    new_values,
    cache_keys,
    cache_values,
    lengths,
    norm_gain,
    draft_weight,
    next_hidden,
):
    chips, cores = lax.axis_size("ch"), lax.axis_size("c")
    chip, core = lax.axis_index("ch"), lax.axis_index("c")
    zh, ny = lax.axis_size("zh"), lax.axis_size("y")
    seqs, steps, feats = queries.shape
    kv_heads, block, head_size = (cache_keys.shape[1], cache_keys.shape[2], cache_keys.shape[3])
    mine = feats // head_size
    width = feats * chips * cores
    half = seqs // cores
    hrows = half * steps
    cols = draft_weight.shape[1]
    other = 1 - core

    packed = queries.reshape(cores, half, steps, mine, head_size).transpose(0, 1, 3, 2, 4)
    packed = packed.reshape(cores, half, mine * steps, head_size)
    spread = jnp.broadcast_to(packed[None], (chips,) + packed.shape)
    spread = spread.reshape((chips * cores,) + packed.shape[1:])

    sib_k = swap(cache_keys)
    sib_v = swap(cache_values)
    sib_w = swap(draft_weight)
    sib_gain = swap(norm_gain)
    sib_hidden = swap(lax.dynamic_slice_in_dim(next_hidden, other * hrows, hrows, 0))
    own_hidden = lax.dynamic_slice_in_dim(next_hidden, core * hrows, hrows, 0)

    heads = lax.all_to_all(spread, TP, 0, 0).reshape(
        kv_heads, cores, half, mine * steps, head_size
    )
    place = (chip * cores + core) * block
    sib_place = (chip * cores + other) * block
    meta = jnp.concatenate([jnp.stack([core, place, sib_place]).astype(jnp.int32), lengths])
    fresh = jnp.stack([new_keys, new_values], axis=1).reshape(
        seqs, 2, steps, kv_heads, head_size
    )
    fresh = fresh.transpose(0, 1, 3, 2, 4).astype(jnp.float32)
    sent = attend(steps, meta, heads, cache_keys, cache_values, sib_k, sib_v, fresh)

    got = lax.all_to_all(sent, "ch", 0, 0)
    q_rows = cores * mine * steps
    outs = got[:, : half * q_rows].astype(jnp.float32).reshape(chips, half, q_rows, head_size)
    lse = got[:, half * q_rows : half * q_rows + 3 * half, :q_rows].astype(jnp.float32)
    lse = jnp.sum(lse.reshape(chips, 3, half, q_rows), axis=1)
    factor = jnp.exp2(lse - jnp.max(lse, axis=0, keepdims=True))
    context = jnp.sum(outs * factor[..., None], axis=0) / jnp.sum(factor, axis=0)[..., None]
    context = context.reshape(half, cores, mine, steps, head_size).transpose(1, 0, 3, 2, 4)
    context = context.reshape(cores, hrows, feats)
    flat_own = lax.dynamic_index_in_dim(context, core, 0, keepdims=False)
    flat_sib = lax.dynamic_index_in_dim(context, other, 0, keepdims=False)
    raw = jnp.stack([flat_own * norm_gain[None, :], flat_sib * sib_gain[None, :]])
    raw = raw.astype(jnp.bfloat16)

    near = jnp.stack([shift(raw, "zh", 1), shift(raw, "zh", 3)])
    far = jnp.stack([raw, shift(raw, "zh", 2)])
    blocks = [near, far]
    for k in (1, 3, 2):
        blocks += [shift(near, "y", k), shift(far, "y", k)]
    row_half = zh * ny * hrows
    row_count = row_half * cores
    where = jnp.stack([lax.axis_index("zh"), lax.axis_index("y")]).astype(jnp.int32)
    partial, own_raw, sib_raw = project(
        where, blocks, norm_gain[None, :], sib_gain[None, :], draft_weight, sib_w
    )
    payload = partial.reshape(chips, cores * hrows, cols + 128)
    oth_raw = swap(sib_raw)
    parts = lax.all_to_all(payload, "ch", 0, 0)
    summed = jnp.sum(parts.astype(jnp.float32), axis=0)
    meansq = jnp.sum(summed[:, cols : cols + 3], axis=1) / width
    scale = lax.rsqrt(meansq + 1e-05)[:, None]
    total = summed[:, :cols] * scale

    flip = core == 1
    hid0 = jnp.where(flip, sib_hidden, own_hidden)
    hid1 = jnp.where(flip, own_hidden, sib_hidden)
    hidden = jnp.concatenate([hid0, hid1]).astype(jnp.float32)
    grad_mine = ((total - hidden) * (scale / math.sqrt(row_count))).astype(jnp.bfloat16)
    pred = total.astype(jnp.bfloat16).reshape(cores, hrows, cols)
    keep = jnp.where(flip, pred[1], pred[0])
    came = swap(jnp.where(flip, pred[0], pred[1]))
    grad_half = gather(grad_mine, "ch").reshape(row_half, cols)
    prediction = jnp.concatenate([jnp.where(flip, came, keep), jnp.where(flip, keep, came)])
    grad_half, prediction = lax.optimization_barrier((grad_half, prediction))
    grad_other = swap(grad_half)

    tn = (((0,), (0,)), ((), ()))
    weight_grad = lax.dot_general(oth_raw, grad_other, tn, preferred_element_type=jnp.float32)
    weight_grad += lax.dot_general(own_raw, grad_half, tn, preferred_element_type=jnp.float32)
    return (prediction, weight_grad.astype(jnp.bfloat16))


def solution(mesh):
    tp, grp = mesh.devices.shape
    fine = Mesh(mesh.devices.reshape(tp // 2, 2, 4, grp // 4), ("ch", "c", "zh", "y"))
    g = ("zh", "y")
    in_specs = (
        P(g, None, TP),
        P(g, None, None),
        P(g, None, None),
        P(g, None, TP, None),
        P(g, None, TP, None),
        P(g),
        P(TP),
        P(TP, g),
        P(TP, g),
    )
    out_specs = (P(TP, g), P(TP, g))
    return jax.shard_map(
        per_device, mesh=fine, in_specs=in_specs, out_specs=out_specs, check_vma=False
    )
```

```python
import functools
import math

import jax
import jax.numpy as jnp
from jax import lax
from jax.experimental import pallas as pl
from jax.experimental.pallas import tpu as pltpu
from jax.sharding import Mesh
from jax.sharding import PartitionSpec as P

TP = ("ch", "c")
TILE = 16


def gather(x, axis):
    n = lax.axis_size(axis)
    return lax.all_to_all(jnp.broadcast_to(x[None], (n,) + x.shape), axis, 0, 0)


def in_hbm(x):
    return pltpu.with_memory_space_constraint(x, pltpu.HBM)


def in_vmem(x):
    return pltpu.with_memory_space_constraint(x, pltpu.VMEM)


def shift(x, axis, k):
    n = lax.axis_size(axis)
    return lax.ppermute(x, axis, [(j, (j + k) % n) for j in range(n)])


def swap(x):
    return lax.ppermute(x, "c", [(0, 1), (1, 0)])


def attend_kernel(
    steps, meta, q_ref, ko, vo, ks, vs, new_ref, sent, buf, out_ref, lse_ref, sems, out_sems
):
    half = buf.shape[1]
    kv_heads, block, head_size = buf.shape[2:]
    q_rows = q_ref.shape[1] * q_ref.shape[3]
    scale = math.log2(math.e) / math.sqrt(head_size)
    core = meta[0]

    def copies(i):
        out = []
        for n, ref in enumerate((ko, ks, vo, vs)):
            src = ref.at[core * half + i]
            out.append(pltpu.make_async_copy(src, buf.at[n, i], sems.at[n, i]))
        return out

    for i in range(half):
        for copy in copies(i):
            copy.start()

    row = lax.broadcasted_iota(jnp.int32, (q_rows, block), 0)
    lane = lax.broadcasted_iota(jnp.int32, (q_rows, block), 1)
    step_of = lax.rem(row, steps) + 1
    column = lax.broadcasted_iota(jnp.int32, (q_rows, 128), 1)
    nt = (((1,), (1,)), ((), ()))
    lse_ref[...] = jnp.zeros_like(lse_ref)

    def one(i):
        length = meta[3 + core * half + i]
        c = copies(i)

        def insert(n, base):
            for j in range(steps):
                place = length + j - base

                @pl.when((place >= 0) & (place < block))
                def _(place=place, j=j):
                    start = pl.multiple_of((place // TILE) * TILE, TILE)
                    hit = lax.broadcasted_iota(jnp.int32, (TILE, head_size), 0) == place - start
                    for k in range(kv_heads):
                        slab = buf[n, i, k, pl.ds(start, TILE), :].astype(jnp.float32)
                        fresh = new_ref[core * half + i, n // 2, k, j : j + 1, :]
                        buf[n, i, k, pl.ds(start, TILE), :] = jnp.where(hit, fresh, slab).astype(
                            jnp.bfloat16
                        )

        c[0].wait()
        c[1].wait()
        insert(0, meta[1])
        insert(1, meta[2])
        limit = length + step_of
        valid_o = lane + meta[1] < limit
        valid_s = lane + meta[2] < limit
        qk = []
        for k in range(kv_heads):
            q = q_ref[k, :, i].reshape(q_rows, head_size)
            so = lax.dot_general(q, buf[0, i, k], nt, preferred_element_type=jnp.float32)
            ss = lax.dot_general(q, buf[1, i, k], nt, preferred_element_type=jnp.float32)
            qk.append((so, ss))
        pr = []
        for k in range(kv_heads):
            so, ss = qk[k]
            so = jnp.where(valid_o, so * scale, -1e30)
            ss = jnp.where(valid_s, ss * scale, -1e30)
            top = jnp.max(jnp.maximum(so, ss), axis=1, keepdims=True)
            po = jnp.exp2(so - top)
            ps = jnp.exp2(ss - top)
            total = jnp.sum(po + ps, axis=1, keepdims=True)
            pr.append((top, total, po.astype(jnp.bfloat16), ps.astype(jnp.bfloat16)))
        c[2].wait()
        c[3].wait()
        insert(2, meta[1])
        insert(3, meta[2])
        for k in range(kv_heads):
            top, total, po, ps = pr[k]
            acc = jnp.dot(po, buf[2, i, k], preferred_element_type=jnp.float32)
            acc += jnp.dot(ps, buf[3, i, k], preferred_element_type=jnp.float32)
            out_ref[k, i * q_rows : (i + 1) * q_rows, :] = (acc / total).astype(jnp.bfloat16)
            lse = jnp.where(top > -1e29, top + jnp.log2(total), -1e30)
            lse_ref[k, :q_rows, :] = jnp.where(column == i, lse, lse_ref[k, :q_rows, :])

    def send(i):
        rows = pl.ds(i * q_rows, q_rows if i < half else TILE)
        return pltpu.make_async_copy(out_ref.at[:, rows], sent.at[:, rows], out_sems.at[i])

    for i in range(half):
        one(i)
        send(i).start()

    for k in range(kv_heads):
        x = lse_ref[k].T[:half]
        a = x.astype(jnp.bfloat16).astype(jnp.float32)
        b = (x - a).astype(jnp.bfloat16).astype(jnp.float32)
        c = x - a - b
        rows = jnp.concatenate([a, b, c, jnp.zeros((TILE - 3 * half, 128), jnp.float32)], 0)
        out_ref[k, half * q_rows :, :] = rows.astype(jnp.bfloat16)
    send(half).start()
    for i in range(half + 1):
        send(i).wait()


def attend(steps, meta, heads, own_k, own_v, sib_k, sib_v, fresh):
    kv_heads, share, half, rows, head_size = heads.shape
    block = own_k.shape[2]
    q_rows = share * rows
    out_rows = half * q_rows + TILE
    vmem = pl.BlockSpec(memory_space=pltpu.VMEM)
    hbm = pl.BlockSpec(memory_space=pl.ANY)
    return pl.pallas_call(
        functools.partial(attend_kernel, steps),
        in_specs=[pl.BlockSpec(memory_space=pltpu.SMEM), vmem, hbm, hbm, hbm, hbm, vmem],
        out_specs=pl.BlockSpec(memory_space=pl.ANY),
        scratch_shapes=[
            pltpu.VMEM((4, half, kv_heads, block, head_size), jnp.bfloat16),
            pltpu.VMEM((kv_heads, out_rows, head_size), jnp.bfloat16),
            pltpu.VMEM((kv_heads, 128, 128), jnp.float32),
            pltpu.SemaphoreType.DMA((4, half)),
            pltpu.SemaphoreType.DMA((half + 1,)),
        ],
        out_shape=pltpu.HBM((kv_heads, out_rows, head_size), jnp.bfloat16),
        compiler_params=pltpu.CompilerParams(vmem_limit_bytes=28 * 1024 * 1024),
        cost_estimate=pl.CostEstimate(
            flops=half * kv_heads * q_rows * 2 * block * head_size * 4,
            bytes_accessed=half * kv_heads * block * head_size * 8,
            transcendentals=half * kv_heads * q_rows * 2 * block,
        ),
        name="attend",
    )(meta, heads, *map(in_hbm, (own_k, own_v, sib_k, sib_v)), fresh)


def project_kernel(tile, place, *refs):
    blocks, refs = refs[:-11], refs[-11:]
    g_own, g_sib, w_own, w_sib, sent, own_out, sib_out = refs[:7]
    own_ref, sib_ref, out_ref, sems = refs[7:]
    hrows = blocks[0].shape[2]
    feats, cols = w_own.shape
    for n, ref in enumerate(blocks):
        y_back, z_backs = (0, 1, 3, 2)[n // 2], ((1, 3), (0, 2))[n % 2]
        y = lax.rem(place[1] - y_back + 4, 4)
        for at, z_back in enumerate(z_backs):
            z = lax.rem(place[0] - z_back + 4, 4)
            rows = pl.ds(pl.multiple_of((z * 4 + y) * hrows, hrows), hrows)
            own_ref[rows, :] = ref[at, 0]
            sib_ref[rows, :] = ref[at, 1]
    copies = [
        pltpu.make_async_copy(own_ref, own_out, sems.at[0]),
        pltpu.make_async_copy(sib_ref, sib_out, sems.at[1]),
    ]
    for copy in copies:
        copy.start()
    def send(n, start, size):
        cut = pl.ds(start, size)
        copy = pltpu.make_async_copy(out_ref.at[:, cut], sent.at[:, cut], sems.at[n])
        copy.start()
        copies.append(copy)

    own, sib = own_ref[...], sib_ref[...]
    for t in range(0, cols, tile):
        acc = jnp.dot(own, w_own[:, t : t + tile], preferred_element_type=jnp.float32)
        acc += jnp.dot(sib, w_sib[:, t : t + tile], preferred_element_type=jnp.float32)
        out_ref[:, t : t + tile] = acc.astype(jnp.bfloat16)
        if t + tile < cols:
            send(2 + t // tile, t, tile)
    sq = 0.0
    for t in range(0, feats, 128):
        a = own_ref[:, t : t + 128].astype(jnp.float32) * (1.0 / g_own[:, t : t + 128])
        b = sib_ref[:, t : t + 128].astype(jnp.float32) * (1.0 / g_sib[:, t : t + 128])
        sq = sq + a * a + b * b
    sq = jnp.sum(sq, axis=1, keepdims=True)
    a = sq.astype(jnp.bfloat16).astype(jnp.float32)
    b = (sq - a).astype(jnp.bfloat16).astype(jnp.float32)
    lane = lax.broadcasted_iota(jnp.int32, (sq.shape[0], 128), 1)
    pieces = jnp.where(lane == 0, a, jnp.where(lane == 1, b, sq - a - b))
    out_ref[:, cols:] = jnp.where(lane < 3, pieces, 0.0).astype(jnp.bfloat16)
    last = cols - tile
    send(2 + last // tile, last, tile + 128)
    for copy in copies:
        copy.wait()


def project(place, blocks, g_own, g_sib, w_own, w_sib):
    hrows, feats = blocks[0].shape[2:]
    cols = w_own.shape[1]
    rows = 16 * hrows
    vmem = pl.BlockSpec(memory_space=pltpu.VMEM)
    hbm = pl.BlockSpec(memory_space=pl.ANY)
    outs = (
        pltpu.HBM((rows, cols + 128), jnp.bfloat16),
        pltpu.HBM((rows, feats), jnp.bfloat16),
        pltpu.HBM((rows, feats), jnp.bfloat16),
    )
    return pl.pallas_call(
        functools.partial(project_kernel, 256),
        in_specs=[pl.BlockSpec(memory_space=pltpu.SMEM)] + [vmem] * (len(blocks) + 4),
        out_specs=(hbm, hbm, hbm),
        scratch_shapes=[
            pltpu.VMEM((rows, feats), jnp.bfloat16),
            pltpu.VMEM((rows, feats), jnp.bfloat16),
            pltpu.VMEM((rows, cols + 128), jnp.bfloat16),
            pltpu.SemaphoreType.DMA((2 + cols // 256,)),
        ],
        out_shape=outs,
        compiler_params=pltpu.CompilerParams(vmem_limit_bytes=24 * 1024 * 1024),
        cost_estimate=pl.CostEstimate(
            flops=rows * feats * cols * 4, bytes_accessed=feats * cols * 4, transcendentals=0
        ),
        name="project",
    )(place, *map(in_vmem, blocks), g_own, g_sib, in_vmem(w_own), in_vmem(w_sib))


def per_device(
    queries,
    new_keys,
    new_values,
    cache_keys,
    cache_values,
    lengths,
    norm_gain,
    draft_weight,
    next_hidden,
):
    chips, cores = lax.axis_size("ch"), lax.axis_size("c")
    chip, core = lax.axis_index("ch"), lax.axis_index("c")
    zh, ny = lax.axis_size("zh"), lax.axis_size("y")
    seqs, steps, feats = queries.shape
    kv_heads, block, head_size = (cache_keys.shape[1], cache_keys.shape[2], cache_keys.shape[3])
    mine = feats // head_size
    width = feats * chips * cores
    half = seqs // cores
    hrows = half * steps
    cols = draft_weight.shape[1]
    other = 1 - core

    packed = queries.reshape(cores, half, steps, mine, head_size).transpose(0, 1, 3, 2, 4)
    packed = packed.reshape(cores, half, mine * steps, head_size)
    spread = jnp.broadcast_to(packed[None], (chips,) + packed.shape)
    spread = spread.reshape((chips * cores,) + packed.shape[1:])

    sib_k = swap(cache_keys)
    sib_v = swap(cache_values)
    sib_w = swap(draft_weight)
    sib_gain = swap(norm_gain)
    sib_hidden = swap(lax.dynamic_slice_in_dim(next_hidden, other * hrows, hrows, 0))
    own_hidden = lax.dynamic_slice_in_dim(next_hidden, core * hrows, hrows, 0)

    heads = lax.all_to_all(spread, TP, 0, 0).reshape(
        kv_heads, cores, half, mine * steps, head_size
    )
    place = (chip * cores + core) * block
    sib_place = (chip * cores + other) * block
    meta = jnp.concatenate([jnp.stack([core, place, sib_place]).astype(jnp.int32), lengths])
    fresh = jnp.stack([new_keys, new_values], axis=1).reshape(
        seqs, 2, steps, kv_heads, head_size
    )
    fresh = fresh.transpose(0, 1, 3, 2, 4).astype(jnp.float32)
    sent = attend(steps, meta, heads, cache_keys, cache_values, sib_k, sib_v, fresh)

    got = lax.all_to_all(sent, "ch", 0, 0)
    q_rows = cores * mine * steps
    outs = got[:, : half * q_rows].astype(jnp.float32).reshape(chips, half, q_rows, head_size)
    lse = got[:, half * q_rows : half * q_rows + 3 * half, :q_rows].astype(jnp.float32)
    lse = jnp.sum(lse.reshape(chips, 3, half, q_rows), axis=1)
    factor = jnp.exp2(lse - jnp.max(lse, axis=0, keepdims=True))
    context = jnp.sum(outs * factor[..., None], axis=0) / jnp.sum(factor, axis=0)[..., None]
    context = context.reshape(half, cores, mine, steps, head_size).transpose(1, 0, 3, 2, 4)
    context = context.reshape(cores, hrows, feats)
    flat_own = lax.dynamic_index_in_dim(context, core, 0, keepdims=False)
    flat_sib = lax.dynamic_index_in_dim(context, other, 0, keepdims=False)
    raw = jnp.stack([flat_own * norm_gain[None, :], flat_sib * sib_gain[None, :]])
    raw = raw.astype(jnp.bfloat16)

    near = jnp.stack([shift(raw, "zh", 1), shift(raw, "zh", 3)])
    far = jnp.stack([raw, shift(raw, "zh", 2)])
    blocks = [near, far]
    for k in (1, 3, 2):
        blocks += [shift(near, "y", k), shift(far, "y", k)]
    row_half = zh * ny * hrows
    row_count = row_half * cores
    where = jnp.stack([lax.axis_index("zh"), lax.axis_index("y")]).astype(jnp.int32)
    partial, own_raw, sib_raw = project(
        where, blocks, norm_gain[None, :], sib_gain[None, :], draft_weight, sib_w
    )
    payload = partial.reshape(chips, cores * hrows, cols + 128)
    oth_raw = swap(sib_raw)
    parts = lax.all_to_all(payload, "ch", 0, 0)
    summed = jnp.sum(parts.astype(jnp.float32), axis=0)
    meansq = jnp.sum(summed[:, cols : cols + 3], axis=1) / width
    scale = lax.rsqrt(meansq + 1e-05)[:, None]
    total = summed[:, :cols] * scale

    flip = core == 1
    hid0 = jnp.where(flip, sib_hidden, own_hidden)
    hid1 = jnp.where(flip, own_hidden, sib_hidden)
    hidden = jnp.concatenate([hid0, hid1]).astype(jnp.float32)
    grad_mine = ((total - hidden) * (scale / math.sqrt(row_count))).astype(jnp.bfloat16)
    pred = total.astype(jnp.bfloat16).reshape(cores, hrows, cols)
    keep = jnp.where(flip, pred[1], pred[0])
    came = swap(jnp.where(flip, pred[0], pred[1]))
    grad_half = gather(grad_mine, "ch").reshape(row_half, cols)
    prediction = jnp.concatenate([jnp.where(flip, came, keep), jnp.where(flip, keep, came)])
    grad_half, prediction = lax.optimization_barrier((grad_half, prediction))
    grad_other = swap(grad_half)

    tn = (((0,), (0,)), ((), ()))
    weight_grad = lax.dot_general(oth_raw, grad_other, tn, preferred_element_type=jnp.float32)
    weight_grad += lax.dot_general(own_raw, grad_half, tn, preferred_element_type=jnp.float32)
    return (prediction, weight_grad.astype(jnp.bfloat16))


def solution(mesh):
    tp, grp = mesh.devices.shape
    fine = Mesh(mesh.devices.reshape(tp // 2, 2, 4, grp // 4), ("ch", "c", "zh", "y"))
    g = ("zh", "y")
    in_specs = (
        P(g, None, TP),
        P(g, None, None),
        P(g, None, None),
        P(g, None, TP, None),
        P(g, None, TP, None),
        P(g),
        P(TP),
        P(TP, g),
        P(TP, g),
    )
    out_specs = (P(TP, g), P(TP, g))
    return jax.shard_map(
        per_device, mesh=fine, in_specs=in_specs, out_specs=out_specs, check_vma=False
    )
```

```python
import functools
import math

import jax
import jax.numpy as jnp
from jax import lax
from jax.experimental import pallas as pl
from jax.experimental.pallas import tpu as pltpu
from jax.sharding import Mesh
from jax.sharding import PartitionSpec as P

TP = ("ch", "c")
TILE = 16


def gather(x, axis):
    n = lax.axis_size(axis)
    return lax.all_to_all(jnp.broadcast_to(x[None], (n,) + x.shape), axis, 0, 0)


def in_hbm(x):
    return pltpu.with_memory_space_constraint(x, pltpu.HBM)


def in_vmem(x):
    return pltpu.with_memory_space_constraint(x, pltpu.VMEM)


def shift(x, axis, k):
    n = lax.axis_size(axis)
    return lax.ppermute(x, axis, [(j, (j + k) % n) for j in range(n)])


def swap(x):
    return lax.ppermute(x, "c", [(0, 1), (1, 0)])


def attend_kernel(
    steps, meta, q_ref, ko, vo, ks, vs, new_ref, sent, buf, out_ref, lse_ref, sems, out_sems
):
    half = buf.shape[1]
    kv_heads, block, head_size = buf.shape[2:]
    q_rows = q_ref.shape[1] * q_ref.shape[3]
    scale = math.log2(math.e) / math.sqrt(head_size)
    core = meta[0]

    def copies(i):
        out = []
        for n, ref in enumerate((ko, ks, vo, vs)):
            src = ref.at[core * half + i]
            out.append(pltpu.make_async_copy(src, buf.at[n, i], sems.at[n, i]))
        return out

    for i in range(half):
        for copy in copies(i):
            copy.start()

    row = lax.broadcasted_iota(jnp.int32, (q_rows, block), 0)
    lane = lax.broadcasted_iota(jnp.int32, (q_rows, block), 1)
    step_of = lax.rem(row, steps) + 1
    column = lax.broadcasted_iota(jnp.int32, (q_rows, 128), 1)
    nt = (((1,), (1,)), ((), ()))
    lse_ref[...] = jnp.zeros_like(lse_ref)

    def one(i):
        length = meta[3 + core * half + i]
        c = copies(i)

        def insert(n, base):
            for j in range(steps):
                place = length + j - base

                @pl.when((place >= 0) & (place < block))
                def _(place=place, j=j):
                    start = pl.multiple_of((place // TILE) * TILE, TILE)
                    hit = lax.broadcasted_iota(jnp.int32, (TILE, head_size), 0) == place - start
                    for k in range(kv_heads):
                        slab = buf[n, i, k, pl.ds(start, TILE), :].astype(jnp.float32)
                        fresh = new_ref[core * half + i, n // 2, k, j : j + 1, :]
                        buf[n, i, k, pl.ds(start, TILE), :] = jnp.where(hit, fresh, slab).astype(
                            jnp.bfloat16
                        )

        c[0].wait()
        c[1].wait()
        insert(0, meta[1])
        insert(1, meta[2])
        limit = length + step_of
        valid_o = lane + meta[1] < limit
        valid_s = lane + meta[2] < limit
        qk = []
        for k in range(kv_heads):
            q = q_ref[k, :, i].reshape(q_rows, head_size)
            so = lax.dot_general(q, buf[0, i, k], nt, preferred_element_type=jnp.float32)
            ss = lax.dot_general(q, buf[1, i, k], nt, preferred_element_type=jnp.float32)
            qk.append((so, ss))
        pr = []
        for k in range(kv_heads):
            so, ss = qk[k]
            so = jnp.where(valid_o, so * scale, -1e30)
            ss = jnp.where(valid_s, ss * scale, -1e30)
            top = jnp.max(jnp.maximum(so, ss), axis=1, keepdims=True)
            po = jnp.exp2(so - top)
            ps = jnp.exp2(ss - top)
            total = jnp.sum(po + ps, axis=1, keepdims=True)
            pr.append((top, total, po.astype(jnp.bfloat16), ps.astype(jnp.bfloat16)))
        c[2].wait()
        c[3].wait()
        insert(2, meta[1])
        insert(3, meta[2])
        for k in range(kv_heads):
            top, total, po, ps = pr[k]
            acc = jnp.dot(po, buf[2, i, k], preferred_element_type=jnp.float32)
            acc += jnp.dot(ps, buf[3, i, k], preferred_element_type=jnp.float32)
            out_ref[k, i * q_rows : (i + 1) * q_rows, :] = (acc / total).astype(jnp.bfloat16)
            lse = jnp.where(top > -1e29, top + jnp.log2(total), -1e30)
            lse_ref[k, :q_rows, :] = jnp.where(column == i, lse, lse_ref[k, :q_rows, :])

    def send(i):
        rows = pl.ds(i * q_rows, q_rows if i < half else TILE)
        return pltpu.make_async_copy(out_ref.at[:, rows], sent.at[:, rows], out_sems.at[i])

    for i in range(half):
        one(i)
        send(i).start()

    for k in range(kv_heads):
        x = lse_ref[k].T[:half]
        a = x.astype(jnp.bfloat16).astype(jnp.float32)
        b = (x - a).astype(jnp.bfloat16).astype(jnp.float32)
        c = x - a - b
        rows = jnp.concatenate([a, b, c, jnp.zeros((TILE - 3 * half, 128), jnp.float32)], 0)
        out_ref[k, half * q_rows :, :] = rows.astype(jnp.bfloat16)
    send(half).start()
    for i in range(half + 1):
        send(i).wait()


def attend(steps, meta, heads, own_k, own_v, sib_k, sib_v, fresh):
    kv_heads, share, half, rows, head_size = heads.shape
    block = own_k.shape[2]
    q_rows = share * rows
    out_rows = half * q_rows + TILE
    vmem = pl.BlockSpec(memory_space=pltpu.VMEM)
    hbm = pl.BlockSpec(memory_space=pl.ANY)
    return pl.pallas_call(
        functools.partial(attend_kernel, steps),
        in_specs=[pl.BlockSpec(memory_space=pltpu.SMEM), vmem, hbm, hbm, hbm, hbm, vmem],
        out_specs=pl.BlockSpec(memory_space=pl.ANY),
        scratch_shapes=[
            pltpu.VMEM((4, half, kv_heads, block, head_size), jnp.bfloat16),
            pltpu.VMEM((kv_heads, out_rows, head_size), jnp.bfloat16),
            pltpu.VMEM((kv_heads, 128, 128), jnp.float32),
            pltpu.SemaphoreType.DMA((4, half)),
            pltpu.SemaphoreType.DMA((half + 1,)),
        ],
        out_shape=pltpu.HBM((kv_heads, out_rows, head_size), jnp.bfloat16),
        compiler_params=pltpu.CompilerParams(vmem_limit_bytes=28 * 1024 * 1024),
        cost_estimate=pl.CostEstimate(
            flops=half * kv_heads * q_rows * 2 * block * head_size * 4,
            bytes_accessed=half * kv_heads * block * head_size * 8,
            transcendentals=half * kv_heads * q_rows * 2 * block,
        ),
        name="attend",
    )(meta, heads, *map(in_hbm, (own_k, own_v, sib_k, sib_v)), fresh)


def project_kernel(tile, place, *refs):
    blocks, refs = refs[:-11], refs[-11:]
    g_own, g_sib, w_own, w_sib, sent, own_out, sib_out = refs[:7]
    own_ref, sib_ref, out_ref, sems = refs[7:]
    hrows = blocks[0].shape[2]
    feats, cols = w_own.shape
    for n, ref in enumerate(blocks):
        y_back, z_backs = (0, 1, 3, 2)[n // 2], ((1, 3), (0, 2))[n % 2]
        y = lax.rem(place[1] - y_back + 4, 4)
        for at, z_back in enumerate(z_backs):
            z = lax.rem(place[0] - z_back + 4, 4)
            rows = pl.ds(pl.multiple_of((z * 4 + y) * hrows, hrows), hrows)
            own_ref[rows, :] = ref[at, 0]
            sib_ref[rows, :] = ref[at, 1]
    copies = [
        pltpu.make_async_copy(own_ref, own_out, sems.at[0]),
        pltpu.make_async_copy(sib_ref, sib_out, sems.at[1]),
    ]
    for copy in copies:
        copy.start()
    def send(n, start, size):
        cut = pl.ds(start, size)
        copy = pltpu.make_async_copy(out_ref.at[:, cut], sent.at[:, cut], sems.at[n])
        copy.start()
        copies.append(copy)

    own, sib = own_ref[...], sib_ref[...]
    for t in range(0, cols, tile):
        acc = jnp.dot(own, w_own[:, t : t + tile], preferred_element_type=jnp.float32)
        acc += jnp.dot(sib, w_sib[:, t : t + tile], preferred_element_type=jnp.float32)
        out_ref[:, t : t + tile] = acc.astype(jnp.bfloat16)
        if t + tile < cols:
            send(2 + t // tile, t, tile)
    sq = 0.0
    for t in range(0, feats, 128):
        a = own_ref[:, t : t + 128].astype(jnp.float32) * (1.0 / g_own[:, t : t + 128])
        b = sib_ref[:, t : t + 128].astype(jnp.float32) * (1.0 / g_sib[:, t : t + 128])
        sq = sq + a * a + b * b
    sq = jnp.sum(sq, axis=1, keepdims=True)
    a = sq.astype(jnp.bfloat16).astype(jnp.float32)
    b = (sq - a).astype(jnp.bfloat16).astype(jnp.float32)
    lane = lax.broadcasted_iota(jnp.int32, (sq.shape[0], 128), 1)
    pieces = jnp.where(lane == 0, a, jnp.where(lane == 1, b, sq - a - b))
    out_ref[:, cols:] = jnp.where(lane < 3, pieces, 0.0).astype(jnp.bfloat16)
    last = cols - tile
    send(2 + last // tile, last, tile + 128)
    for copy in copies:
        copy.wait()


def project(place, blocks, g_own, g_sib, w_own, w_sib):
    hrows, feats = blocks[0].shape[2:]
    cols = w_own.shape[1]
    rows = 16 * hrows
    vmem = pl.BlockSpec(memory_space=pltpu.VMEM)
    hbm = pl.BlockSpec(memory_space=pl.ANY)
    outs = (
        pltpu.HBM((rows, cols + 128), jnp.bfloat16),
        pltpu.HBM((rows, feats), jnp.bfloat16),
        pltpu.HBM((rows, feats), jnp.bfloat16),
    )
    return pl.pallas_call(
        functools.partial(project_kernel, 256),
        in_specs=[pl.BlockSpec(memory_space=pltpu.SMEM)] + [vmem] * (len(blocks) + 4),
        out_specs=(hbm, hbm, hbm),
        scratch_shapes=[
            pltpu.VMEM((rows, feats), jnp.bfloat16),
            pltpu.VMEM((rows, feats), jnp.bfloat16),
            pltpu.VMEM((rows, cols + 128), jnp.bfloat16),
            pltpu.SemaphoreType.DMA((2 + cols // 256,)),
        ],
        out_shape=outs,
        compiler_params=pltpu.CompilerParams(vmem_limit_bytes=24 * 1024 * 1024),
        cost_estimate=pl.CostEstimate(
            flops=rows * feats * cols * 4, bytes_accessed=feats * cols * 4, transcendentals=0
        ),
        name="project",
    )(place, *map(in_vmem, blocks), g_own, g_sib, in_vmem(w_own), in_vmem(w_sib))


def per_device(
    queries,
    new_keys,
    new_values,
    cache_keys,
    cache_values,
    lengths,
    norm_gain,
    draft_weight,
    next_hidden,
):
    chips, cores = lax.axis_size("ch"), lax.axis_size("c")
    chip, core = lax.axis_index("ch"), lax.axis_index("c")
    zh, ny = lax.axis_size("zh"), lax.axis_size("y")
    seqs, steps, feats = queries.shape
    kv_heads, block, head_size = (cache_keys.shape[1], cache_keys.shape[2], cache_keys.shape[3])
    mine = feats // head_size
    width = feats * chips * cores
    half = seqs // cores
    hrows = half * steps
    cols = draft_weight.shape[1]
    other = 1 - core

    packed = queries.reshape(cores, half, steps, mine, head_size).transpose(0, 1, 3, 2, 4)
    packed = packed.reshape(cores, half, mine * steps, head_size)
    spread = jnp.broadcast_to(packed[None], (chips,) + packed.shape)
    spread = spread.reshape((chips * cores,) + packed.shape[1:])

    sib_k = swap(cache_keys)
    sib_v = swap(cache_values)
    sib_w = swap(draft_weight)
    sib_gain = swap(norm_gain)
    sib_hidden = swap(lax.dynamic_slice_in_dim(next_hidden, other * hrows, hrows, 0))
    own_hidden = lax.dynamic_slice_in_dim(next_hidden, core * hrows, hrows, 0)

    heads = lax.all_to_all(spread, TP, 0, 0).reshape(
        kv_heads, cores, half, mine * steps, head_size
    )
    place = (chip * cores + core) * block
    sib_place = (chip * cores + other) * block
    meta = jnp.concatenate([jnp.stack([core, place, sib_place]).astype(jnp.int32), lengths])
    fresh = jnp.stack([new_keys, new_values], axis=1).reshape(
        seqs, 2, steps, kv_heads, head_size
    )
    fresh = fresh.transpose(0, 1, 3, 2, 4).astype(jnp.float32)
    sent = attend(steps, meta, heads, cache_keys, cache_values, sib_k, sib_v, fresh)

    got = lax.all_to_all(sent, "ch", 0, 0)
    q_rows = cores * mine * steps
    outs = got[:, : half * q_rows].astype(jnp.float32).reshape(chips, half, q_rows, head_size)
    lse = got[:, half * q_rows : half * q_rows + 3 * half, :q_rows].astype(jnp.float32)
    lse = jnp.sum(lse.reshape(chips, 3, half, q_rows), axis=1)
    factor = jnp.exp2(lse - jnp.max(lse, axis=0, keepdims=True))
    context = jnp.sum(outs * factor[..., None], axis=0) / jnp.sum(factor, axis=0)[..., None]
    context = context.reshape(half, cores, mine, steps, head_size).transpose(1, 0, 3, 2, 4)
    context = context.reshape(cores, hrows, feats)
    flat_own = lax.dynamic_index_in_dim(context, core, 0, keepdims=False)
    flat_sib = lax.dynamic_index_in_dim(context, other, 0, keepdims=False)
    raw = jnp.stack([flat_own * norm_gain[None, :], flat_sib * sib_gain[None, :]])
    raw = raw.astype(jnp.bfloat16)

    z_1, z_3 = shift(raw, "zh", 1), shift(raw, "zh", 3)
    near = jnp.stack([z_1, z_3])
    later, _ = lax.optimization_barrier((raw, z_1))
    far = jnp.stack([raw, shift(later, "zh", 2)])
    blocks = [near, far]
    for k in (1, 3, 2):
        blocks += [shift(near, "y", k), shift(far, "y", k)]
    row_half = zh * ny * hrows
    row_count = row_half * cores
    where = jnp.stack([lax.axis_index("zh"), lax.axis_index("y")]).astype(jnp.int32)
    partial, own_raw, sib_raw = project(
        where, blocks, norm_gain[None, :], sib_gain[None, :], draft_weight, sib_w
    )
    payload = partial.reshape(chips, cores * hrows, cols + 128)
    oth_raw = swap(sib_raw)
    parts = lax.all_to_all(payload, "ch", 0, 0)
    summed = jnp.sum(parts.astype(jnp.float32), axis=0)
    meansq = jnp.sum(summed[:, cols : cols + 3], axis=1) / width
    scale = lax.rsqrt(meansq + 1e-05)[:, None]
    total = summed[:, :cols] * scale

    flip = core == 1
    hid0 = jnp.where(flip, sib_hidden, own_hidden)
    hid1 = jnp.where(flip, own_hidden, sib_hidden)
    hidden = jnp.concatenate([hid0, hid1]).astype(jnp.float32)
    grad_mine = ((total - hidden) * (scale / math.sqrt(row_count))).astype(jnp.bfloat16)
    pred = total.astype(jnp.bfloat16).reshape(cores, hrows, cols)
    keep = jnp.where(flip, pred[1], pred[0])
    came = swap(jnp.where(flip, pred[0], pred[1]))
    grad_half = gather(grad_mine, "ch").reshape(row_half, cols)
    prediction = jnp.concatenate([jnp.where(flip, came, keep), jnp.where(flip, keep, came)])
    grad_half, prediction = lax.optimization_barrier((grad_half, prediction))
    grad_other = swap(grad_half)

    tn = (((0,), (0,)), ((), ()))
    weight_grad = lax.dot_general(oth_raw, grad_other, tn, preferred_element_type=jnp.float32)
    weight_grad += lax.dot_general(own_raw, grad_half, tn, preferred_element_type=jnp.float32)
    return (prediction, weight_grad.astype(jnp.bfloat16))


def solution(mesh):
    tp, grp = mesh.devices.shape
    fine = Mesh(mesh.devices.reshape(tp // 2, 2, 4, grp // 4), ("ch", "c", "zh", "y"))
    g = ("zh", "y")
    in_specs = (
        P(g, None, TP),
        P(g, None, None),
        P(g, None, None),
        P(g, None, TP, None),
        P(g, None, TP, None),
        P(g),
        P(TP),
        P(TP, g),
        P(TP, g),
    )
    out_specs = (P(TP, g), P(TP, g))
    return jax.shard_map(
        per_device, mesh=fine, in_specs=in_specs, out_specs=out_specs, check_vma=False
    )
```
